32 devices in a mesh: cell: 2 (over core), grp: 16 (over z, y, x).
Axes of the slice: x: 2, y: 2, z: 4, core: 2. Of those that a mesh axis runs over, the one named last changes fastest.
Arguments:
- v_free: float32 [3, 262144], P(None, 'grp'), may hold values from -6 to 6
- inv_mass: float32 [262144], P('grp'), may hold values from 0.2 to 5
- pairs: int32 [2, 1024, 128], P(None, ('cell', 'grp')), may hold values from 0 to 20479, as said below
- angles: float32 [2, 1024, 128], P(None, ('cell', 'grp')), may hold values from -3.140625 to 3.140625
- bias: float32 [1024, 128], P(('cell', 'grp')), may hold values from -6 to 6
- friction: float32 [1024, 128], P(('cell', 'grp')), may hold values from 0.2 to 1
- counts: int32 [1024], P(('cell', 'grp')), may hold values from 16 to 128, as said below
Outputs:
- velocity: float32 [3, 262144], P(None, 'grp')
- impulses: float32 [3, 1024, 128], P(None, ('cell', 'grp'))
The draws below stay inside these ranges and needn't reach their ends.
Inputs may be any that keep to these rules, and one draw needn't show every extreme that they name: A spatial cell's window of bodies holds the last 2048 bodies of the previous cell (positions 0 to 2047), the cell's own 16384 bodies (positions 2048 to 18431) and the first 2048 bodies of the next cell (the remaining positions). pairs[0] is always one of the cell's own bodies; pairs[1] is another own body or a rim body of a neighbouring cell. No slot of the first cell names the previous rim and no slot of the last cell names the next rim. `counts`: the first block of each 32 blocks is full.
All inputs are finite; a program needn't handle non-finite values.
Results may differ from the reference program's by a relative error of at most 0.0001.
Values sent between devices are 32-bit elements; how exact they have to be, the bound alone decides.
A program may use at most 128 MiB of HBM per device.

```python
import math
import jax
import jax.numpy as jnp
from jax import lax

B_DEV = 16384
RIM = 2048
BLK_DEV = 32
CONTACTS = 128
ITERS = 3
CELLS = 16
NB = 262144
NBLK = 1024


def draw_pairs(key, part):
    rows = jnp.arange(NBLK, dtype=jnp.int32)[:, None] + jnp.zeros((1, CONTACTS), jnp.int32)
    columns = jnp.arange(CONTACTS, dtype=jnp.int32)[None, :] + jnp.zeros((NBLK, 1), jnp.int32)
    cell_index = rows // BLK_DEV % CELLS
    last_cell = CELLS - 1
    keys = jax.random.split(key, 4)
    kind = jax.random.randint(keys[0], (NBLK, CONTACTS), 0, 4)
    kind = jnp.where((kind == 0) & (cell_index == 0), 2, kind)
    kind = jnp.where((kind == 1) & (cell_index == last_cell), 3, kind)
    at_low = (rows == BLK_DEV) & (columns == 0)
    at_high = (rows == 0) & (columns == 0)
    kind = jnp.where(at_low, 0, jnp.where(at_high, 1, kind))
    local_a = jax.random.randint(keys[1], (NBLK, CONTACTS), 0, B_DEV)
    rim_pick = jax.random.randint(keys[2], (NBLK, CONTACTS), 0, RIM)
    rim_pick = jnp.where(at_low, 0, jnp.where(at_high, RIM - 1, rim_pick))
    other = jax.random.randint(keys[3], (NBLK, CONTACTS), 1, B_DEV)
    first_local = jnp.where(kind == 0, local_a % RIM, jnp.where(kind == 1, B_DEV - 1 - local_a % RIM, local_a))
    second = jnp.where(kind == 0, rim_pick, jnp.where(kind == 1, RIM + B_DEV + rim_pick, RIM + (local_a + other) % B_DEV))
    first = RIM + first_local
    return jnp.stack([first, second]).astype(jnp.int32)


def draw_counts(key, part):
    rows = jnp.arange(NBLK, dtype=jnp.int32)
    cell_index = rows // BLK_DEV % CELLS
    lowest = jnp.where(cell_index % 3 == 0, 96, 16)
    drawn = jax.random.randint(key, (NBLK,), lowest, CONTACTS + 1)
    drawn = jnp.where((rows % BLK_DEV == 1) & (cell_index % 3 != 0), 16, drawn)
    return jnp.where(rows % BLK_DEV == 0, CONTACTS, drawn).astype(jnp.int32)


def steps_of(stream_key, extent, shards, least, largest):
    def one(axis_at, blocks):
        steps = jax.random.uniform(jax.random.fold_in(jax.random.fold_in(stream_key, 6), axis_at), (blocks,), jnp.float32, least / len(shards), largest / len(shards))
        return jnp.repeat(jnp.exp(steps), extent[axis_at] // blocks).reshape((-1,) + (1,) * (len(extent) - axis_at - 1))

    loudness = one(*shards[0])
    for cut in shards[1:]:
        loudness = loudness * one(*cut)
    return loudness


def bell_draw(stream_key, extent, scale, bound, cuts=(), kind=jnp.bfloat16):
    result = jax.random.normal(stream_key, extent, jnp.float32) * scale
    if len(cuts) > 0:
        result = steps_of(stream_key, extent, cuts, -0.22, 0.18) * result
    return jnp.clip(result, min=-bound, max=bound).astype(kind)


def setup_inputs(seed: int = 0) -> dict:
    arg_keys = jax.random.split(jax.random.key(seed), 8)
    return {
        "v_free": bell_draw(arg_keys[0], (3, NB), 1.0, 6.0, ((1, 16),), jnp.float32),
        "inv_mass": jnp.clip(jnp.exp(math.log(5.0) - 3.218876 * jax.random.uniform(arg_keys[1], (NB,), jnp.float32) ** steps_of(arg_keys[1], (NB,), ((0, 16),), -0.2, 0.2)), 0.2, 5.0),
        "pairs": draw_pairs(jax.random.fold_in(arg_keys[7], 71), 0),
        "angles": jnp.clip(jax.random.uniform(arg_keys[3], (2, NBLK, CONTACTS), jnp.float32, -3.140625, 3.140625), -3.140625, 3.140625),
        "bias": bell_draw(arg_keys[4], (NBLK, CONTACTS), 1.0, 6.0, ((0, 32),), jnp.float32),
        "friction": jnp.clip(0.2 + 0.8 * jax.random.uniform(arg_keys[5], (NBLK, CONTACTS), jnp.float32) ** steps_of(arg_keys[5], (NBLK, CONTACTS), ((0, 32),), -0.2, 0.2), 0.2, 1.0),
        "counts": draw_counts(jax.random.fold_in(arg_keys[7], 71), 0),
    }


relax_factor = 0.6
tangent_floor = 0.05

def frames(angles):
    sin_polar = jnp.sin(angles[0])
    cos_polar = jnp.cos(angles[0])
    sin_azim = jnp.sin(angles[1])
    cos_azim = jnp.cos(angles[1])
    normal = jnp.stack([sin_polar * cos_azim, sin_polar * sin_azim, cos_polar])
    first_tan = jnp.stack([cos_polar * cos_azim, cos_polar * sin_azim, -sin_polar])
    second_tan = jnp.stack([-sin_azim, cos_azim, jnp.zeros_like(sin_azim)])
    return (normal, first_tan, second_tan)

def contact_update(relative, lambdas, normal, first_tan, second_tan, reduced, bias, friction, active):
    speed_n = lax.optimization_barrier(jnp.sum(normal * relative, axis=0)) + bias
    speed_a = lax.optimization_barrier(jnp.sum(first_tan * relative, axis=0))
    speed_b = lax.optimization_barrier(jnp.sum(second_tan * relative, axis=0))
    trial_n = lambdas[0] - relax_factor * reduced * speed_n
    trial_a = lambdas[1] - relax_factor * reduced * speed_a
    trial_b = lambdas[2] - relax_factor * reduced * speed_b
    normal_imp = jnp.maximum(trial_n, 0.0)
    tan_size = jnp.sqrt(trial_a * trial_a + trial_b * trial_b)
    factor = jnp.minimum(1.0, friction * normal_imp / jnp.maximum(tan_size, tangent_floor))
    fresh = jnp.stack([normal_imp, trial_a * factor, trial_b * factor]) * active[None]
    force = normal * fresh[0] + first_tan * fresh[1] + second_tan * fresh[2]
    return (fresh, force)

def reference(v_free, inv_mass, pairs, angles, bias, friction, counts):
    block_rows = jnp.arange(bias.shape[0], dtype=jnp.int32)
    cell_of = block_rows // BLK_DEV % CELLS
    offset = (cell_of * B_DEV - RIM).astype(jnp.int32)[:, None]
    first = (pairs[0] + offset).astype(jnp.int32)
    second = (pairs[1] + offset).astype(jnp.int32)
    slots = jnp.arange(bias.shape[1], dtype=jnp.int32)
    active = (slots[None, :] < counts[:, None]).astype(jnp.float32)
    normal, first_tan, second_tan = frames(angles)
    reduced = 1.0 / (inv_mass[first] + inv_mass[second])
    lambdas = jnp.zeros((3,) + bias.shape, jnp.float32)
    velocity = v_free
    for sweep in range(ITERS):
        relative = velocity[:, first] - velocity[:, second]
        lambdas, force = contact_update(relative, lambdas, normal, first_tan, second_tan, reduced, bias, friction, active)
        total = jnp.zeros_like(v_free).at[:, first].add(force).at[:, second].add(-force)
        velocity = v_free + inv_mass[None, :] * total
    return (velocity, lambdas)
```

```python
import functools

import jax
import jax.numpy as jnp
from jax import lax
from jax.experimental import pallas as pl
from jax.experimental.pallas import tpu as pltpu
from jax.sharding import PartitionSpec as P

RIM = 2048
ITERS = 3
LANES = 128

relax_factor = 0.6
tangent_floor = 0.05


def split_terms(value):
    high = value.astype(jnp.bfloat16)
    low = (value - high.astype(jnp.float32)).astype(jnp.bfloat16)
    return high, low


def kernel(
    cells,
    counts_ref, v_ref, mass_ref, pairs_ref, angles_ref, bias_ref, friction_ref,
    vel_out, imp_out,
    hot1, hot2, row1, row2, active,
    h1_ref, h2_ref, l1_ref, l2_ref,
    vb, vfree_all, mass_all, rel, force_ref, acc,
    edge_out, edge_in, totals, sib_in, bound_out, bound_in,
    edge_send, edge_recv, sib_send, sib_recv, bound_send, bound_recv,
):
    rows = v_ref.shape[1]
    rim = RIM // LANES
    half = rows // 2
    deep = half + rim
    tiles = pairs_ref.shape[1] // 8
    core = lax.axis_index("cell")
    cell = lax.axis_index("grp")
    has_prev = cell > 0
    has_next = cell < cells - 1
    present = (has_prev, has_next)
    steps = (-1, 1)

    barrier = pltpu.get_barrier_semaphore()
    pl.semaphore_signal(barrier, inc=1, device_id={"cell": 1 - core}, device_id_type=pl.DeviceIdType.MESH)
    for side in range(2):
        @pl.when(present[side])
        def _():
            pl.semaphore_signal(
                barrier, inc=1, device_id={"grp": cell + steps[side]}, device_id_type=pl.DeviceIdType.MESH
            )

    edge_out[0, 0:3] = v_ref[:, 0:rim]
    edge_out[0, 3] = mass_ref[0:rim]
    edge_out[1, 0:3] = v_ref[:, rows - rim:rows]
    edge_out[1, 3] = mass_ref[rows - rim:rows]
    for side in range(2):
        @pl.when(jnp.logical_not(present[side]))
        def _():
            edge_in[side] = jnp.zeros(edge_in.shape[1:], jnp.float32)
            for sweep in range(ITERS):
                bound_in[sweep, side] = jnp.zeros(bound_in.shape[2:], jnp.float32)

    inner = jnp.logical_and(has_prev, has_next)

    @pl.when(inner)
    def _():
        pl.semaphore_wait(barrier, 3)

    @pl.when(jnp.logical_not(inner))
    def _():
        pl.semaphore_wait(barrier, 2)

    def edge_copy(side):
        return pltpu.make_async_remote_copy(
            src_ref=edge_out.at[side], dst_ref=edge_in.at[1 - side],
            send_sem=edge_send.at[side], recv_sem=edge_recv.at[1 - side],
            device_id={"grp": cell + steps[side]}, device_id_type=pl.DeviceIdType.MESH,
        )

    def sib_copy(sweep):
        return pltpu.make_async_remote_copy(
            src_ref=totals.at[sweep], dst_ref=sib_in.at[sweep],
            send_sem=sib_send.at[sweep], recv_sem=sib_recv.at[sweep],
            device_id={"cell": 1 - core}, device_id_type=pl.DeviceIdType.MESH,
        )

    def bound_copy(sweep, side):
        return pltpu.make_async_remote_copy(
            src_ref=bound_out.at[sweep, side], dst_ref=bound_in.at[sweep, 1 - side],
            send_sem=bound_send.at[sweep, side], recv_sem=bound_recv.at[sweep, 1 - side],
            device_id={"grp": cell + steps[side]}, device_id_type=pl.DeviceIdType.MESH,
        )

    for side in range(2):
        @pl.when(present[side])
        def _():
            edge_copy(side).start()

    def place(position):
        own = position - RIM
        r = own >> 7
        lane = own & (LANES - 1)
        upper = r >= half
        h = jnp.where(upper, jnp.where(r >= rows - rim, r - (rows - rim), r - (half - rim)), r)
        l = jnp.where(upper, LANES, 0) + lane
        before = position < RIM
        after = own >= rows * LANES
        h = jnp.where(before, half + (position >> 7), jnp.where(after, half + r - rows, h))
        l = jnp.where(before, lane, jnp.where(after, LANES + lane, l))
        return h, l

    h1_ref[...], l1_ref[...] = place(pairs_ref[0])
    h2_ref[...], l2_ref[...] = place(pairs_ref[1])

    slot = lax.broadcasted_iota(jnp.int32, (1, LANES), 1)
    for r in range(pairs_ref.shape[1]):
        active[r:r + 1, :] = jnp.where(slot < counts_ref[r], 1.0, 0.0)

    def pair_row(tile, u):
        return jnp.concatenate([tile[2 * u:2 * u + 1], tile[2 * u + 1:2 * u + 2]], axis=1)

    wide = 2 * LANES
    iota_l = lax.broadcasted_iota(jnp.int32, (wide, wide), 0)
    iota_h = lax.broadcasted_iota(jnp.int32, (half, wide), 0)
    iota_r = lax.broadcasted_iota(jnp.int32, (rim, wide), 0) + half

    @pl.loop(0, tiles)
    def _(i):
        at = pl.ds(pl.multiple_of(i * 8, 8), 8)
        l1, l2, h1, h2 = l1_ref[at, :], l2_ref[at, :], h1_ref[at, :], h2_ref[at, :]
        for u in range(4):
            cut = slice(u * wide, (u + 1) * wide)
            hot1[i, :, cut] = jnp.where(iota_l == pair_row(l1, u), 1.0, 0.0).astype(jnp.bfloat16)
            hot2[i, :, cut] = jnp.where(iota_l == pair_row(l2, u), 1.0, 0.0).astype(jnp.bfloat16)
            row1[i, :, cut] = jnp.where(iota_h == pair_row(h1, u), 1.0, 0.0).astype(jnp.bfloat16)
            row2[i, 0:half, cut] = jnp.where(iota_h == pair_row(h2, u), 1.0, 0.0).astype(jnp.bfloat16)
            row2[i, half:deep, cut] = jnp.where(iota_r == pair_row(h2, u), 1.0, 0.0).astype(jnp.bfloat16)

    sin_p, cos_p = jnp.sin(angles_ref[0]), jnp.cos(angles_ref[0])
    sin_q, cos_q = jnp.sin(angles_ref[1]), jnp.cos(angles_ref[1])
    normal = (sin_p * cos_q, sin_p * sin_q, cos_p)
    first_tan = (cos_p * cos_q, cos_p * sin_q, -sin_p)
    second_tan = (-sin_q, cos_q)

    def fold(block):
        lower = block[..., 0:half, :]
        upper = jnp.concatenate([block[..., rows - rim:rows, :], block[..., half:rows - rim, :]], axis=-2)
        return jnp.concatenate([lower, upper], axis=-1)

    vfree_all[:, 0:half] = fold(v_ref[...])
    mass_all[0:half] = fold(mass_ref[...])
    for side in range(2):
        @pl.when(present[side])
        def _():
            edge_copy(1 - side).wait_recv()
    for side in range(2):
        cut = slice(side * LANES, (side + 1) * LANES)
        vfree_all[:, half:deep, cut] = edge_in[side, 0:3]
        mass_all[half:deep, cut] = edge_in[side, 3]

    def store_terms(parts, count):
        for c, part in enumerate(parts):
            for t, term in enumerate(split_terms(part)):
                at = (t * count + c) * half
                vb[at:at + half, :] = term[0:half]
                at = 2 * count * half + (t * count + c) * rim
                vb[at:at + rim, :] = term[half:deep]

    def gather(count):
        own = 2 * count * half
        whole = 2 * count * deep

        @pl.loop(0, tiles)
        def _(i):
            at = pl.ds(pl.multiple_of(i * 8, 8), 8)
            h1, h2 = h1_ref[at, :], h2_ref[at, :]
            found = [[] for _ in range(count)]
            for u in range(4):
                cut = slice(u * wide, (u + 1) * wide)
                g1 = jnp.dot(vb[0:own, :], hot1[i, :, cut], preferred_element_type=jnp.float32)
                g2 = jnp.dot(vb[0:whole, :], hot2[i, :, cut], preferred_element_type=jnp.float32)
                at1, at2 = iota_h == pair_row(h1, u), iota_h == pair_row(h2, u)
                at_rim = iota_r == pair_row(h2, u)
                for c in range(count):
                    def both(g, base, size):
                        a = base + c * size
                        b = a + count * size
                        return g[a:a + size] + g[b:b + size]
                    first = jnp.where(at1, both(g1, 0, half), 0.0)
                    second = jnp.where(at2, both(g2, 0, half), 0.0)
                    outer = jnp.where(at_rim, both(g2, own, rim), 0.0)
                    first = jnp.sum(first.reshape(half // 8, 8, wide), axis=0)
                    second = jnp.sum(second.reshape(half // 8, 8, wide), axis=0)
                    second += jnp.sum(outer.reshape(rim // 8, 8, wide), axis=0)
                    both_ends = first + second if c == 3 else first - second
                    line = jnp.sum(both_ends, axis=0, keepdims=True)
                    found[c] += [line[:, 0:LANES], line[:, LANES:wide]]
            for c in range(count):
                rel[c, at, :] = jnp.concatenate(found[c], axis=0)

    def scatter():
        acc[...] = jnp.zeros(acc.shape, jnp.float32)
        contract = (((1,), (1,)), ((), ()))

        @pl.loop(0, tiles)
        def _(i):
            at = pl.ds(pl.multiple_of(i * 8, 8), 8)
            pieces = []
            for c in range(3):
                tile = force_ref[c, at, :]
                wide_row = jnp.concatenate([tile[s:s + 1] for s in range(8)], axis=1)
                spread = jnp.broadcast_to(wide_row, (16, 8 * LANES))
                pieces.append(split_terms(spread))

            def weigh(mask, sign):
                size = mask.shape[0]
                done = []
                for t in range(2):
                    for c in range(3):
                        block = mask.reshape(size // 16, 16, 8 * LANES) * (sign * pieces[c][t])[None]
                        done.append(block.reshape(size, 8 * LANES))
                return done

            mine = jnp.concatenate(weigh(row1[i], 1), axis=0)
            mask2 = row2[i]
            theirs = jnp.concatenate(weigh(mask2[0:half], -1) + weigh(mask2[half:deep], -1), axis=0)
            acc[0:6 * half, :] += lax.dot_general(mine, hot1[i], contract, preferred_element_type=jnp.float32)
            acc[...] += lax.dot_general(theirs, hot2[i], contract, preferred_element_type=jnp.float32)

    lambdas = [jnp.zeros(bias_ref.shape, jnp.float32)] * 3
    velocity = [vfree_all[c] for c in range(3)]
    reduced = None
    for sweep in range(ITERS):
        last = sweep == ITERS - 1
        if sweep == 0:
            store_terms(velocity + [mass_all[...]], 4)
            gather(4)
            reduced = relax_factor / rel[3]
        else:
            store_terms(velocity, 3)
            gather(3)
        x, y, z = rel[0], rel[1], rel[2]
        speed_n = normal[0] * x + normal[1] * y + normal[2] * z + bias_ref[...]
        speed_a = first_tan[0] * x + first_tan[1] * y + first_tan[2] * z
        speed_b = second_tan[0] * x + second_tan[1] * y
        trial_n = lambdas[0] - reduced * speed_n
        trial_a = lambdas[1] - reduced * speed_a
        trial_b = lambdas[2] - reduced * speed_b
        normal_imp = jnp.maximum(trial_n, 0.0)
        tan_size = jnp.sqrt(trial_a * trial_a + trial_b * trial_b)
        factor = jnp.minimum(1.0, friction_ref[...] * normal_imp / jnp.maximum(tan_size, tangent_floor))
        live = active[...]
        lambdas = [normal_imp * live, trial_a * factor * live, trial_b * factor * live]
        for c in range(3):
            force = normal[c] * lambdas[0] + first_tan[c] * lambdas[1]
            if c < 2:
                force = force + second_tan[c] * lambdas[2]
            force_ref[c] = force
        scatter()
        for c in range(3):
            for base, size, start in ((0, half, 0), (6 * half, rim, half)):
                a = base + c * size
                b = a + 3 * size
                totals[sweep, c, start:start + size] = acc[a:a + size, :] + acc[b:b + size, :]
        sib_copy(sweep).start()
        sib_copy(sweep).wait_recv()
        total = totals[sweep] + sib_in[sweep]
        for side in range(2):
            cut = slice(side * LANES, (side + 1) * LANES)
            bound_out[sweep, side, :, 0:rim] = total[:, 0:rim, cut]
            bound_out[sweep, side, :, rim:2 * rim] = total[:, half:deep, cut]
        for side in range(2):
            @pl.when(present[side])
            def _():
                bound_copy(sweep, side).start()
        for side in range(2):
            @pl.when(present[side])
            def _():
                bound_copy(sweep, 1 - side).wait_recv()
        near = jnp.concatenate([bound_in[sweep, s, :, rim:2 * rim] for s in range(2)], axis=-1)
        velocity = []
        far = None if last else jnp.concatenate([bound_in[sweep, s, :, 0:rim] for s in range(2)], axis=-1)
        for c in range(3):
            parts = [total[c, 0:rim] + near[c], total[c, rim:half]]
            if not last:
                parts.append(total[c, half:deep] + far[c])
            part = jnp.concatenate(parts, axis=0)
            size = half if last else deep
            velocity.append(vfree_all[c, 0:size] + mass_all[0:size] * part)
    for c in range(3):
        vel_out[c, 0:half] = velocity[c][:, 0:LANES]
        vel_out[c, half:rows - rim] = velocity[c][rim:half, LANES:wide]
        vel_out[c, rows - rim:rows] = velocity[c][0:rim, LANES:wide]
        imp_out[c] = lambdas[c]
    for side in range(2):
        @pl.when(present[side])
        def _():
            edge_copy(side).wait_send()
            for sweep in range(ITERS):
                bound_copy(sweep, side).wait_send()
    for sweep in range(ITERS):
        sib_copy(sweep).wait_send()


def on_device(cells, v_free, inv_mass, pairs, angles, bias, friction, counts):
    width = v_free.shape[1]
    blocks, slots = bias.shape
    rows = width // LANES
    rim = RIM // LANES
    half = rows // 2
    deep = half + rim
    tiles = blocks // 8
    wide = 2 * LANES
    f32, bf16, i32 = jnp.float32, jnp.bfloat16, jnp.int32
    vmem = pl.BlockSpec(memory_space=pltpu.VMEM)
    dma = pltpu.SemaphoreType.DMA
    velocity, impulses = pl.pallas_call(
        functools.partial(kernel, cells),
        out_shape=(
            jax.ShapeDtypeStruct((3, rows, LANES), f32),
            jax.ShapeDtypeStruct((3, blocks, slots), f32),
        ),
        in_specs=[pl.BlockSpec(memory_space=pltpu.SMEM)] + [vmem] * 6,
        out_specs=(vmem, vmem),
        scratch_shapes=[
            pltpu.VMEM((tiles, wide, 8 * LANES), bf16),
            pltpu.VMEM((tiles, wide, 8 * LANES), bf16),
            pltpu.VMEM((tiles, half, 8 * LANES), bf16),
            pltpu.VMEM((tiles, deep, 8 * LANES), bf16),
            pltpu.VMEM((blocks, slots), f32),
            pltpu.VMEM((blocks, slots), i32),
            pltpu.VMEM((blocks, slots), i32),
            pltpu.VMEM((blocks, slots), i32),
            pltpu.VMEM((blocks, slots), i32),
            pltpu.VMEM((8 * deep, wide), bf16),
            pltpu.VMEM((3, deep, wide), f32),
            pltpu.VMEM((deep, wide), f32),
            pltpu.VMEM((4, blocks, slots), f32),
            pltpu.VMEM((3, blocks, slots), f32),
            pltpu.VMEM((6 * deep, wide), f32),
            pltpu.VMEM((2, 4, rim, LANES), f32),
            pltpu.VMEM((2, 4, rim, LANES), f32),
            pltpu.VMEM((ITERS, 3, deep, wide), f32),
            pltpu.VMEM((ITERS, 3, deep, wide), f32),
            pltpu.VMEM((ITERS, 2, 3, 2 * rim, LANES), f32),
            pltpu.VMEM((ITERS, 2, 3, 2 * rim, LANES), f32),
            dma((2,)),
            dma((2,)),
            dma((ITERS,)),
            dma((ITERS,)),
            dma((ITERS, 2)),
            dma((ITERS, 2)),
        ],
        compiler_params=pltpu.CompilerParams(
            collective_id=0, has_side_effects=True, vmem_limit_bytes=40 * 1024 * 1024
        ),
    )(
        counts,
        v_free.reshape(3, rows, LANES),
        inv_mass.reshape(rows, LANES),
        pairs, angles, bias, friction,
    )
    return velocity.reshape(3, width), impulses


def solution(mesh):
    return jax.shard_map(
        functools.partial(on_device, mesh.shape["grp"]),
        mesh=mesh,
        in_specs=(
            P(None, "grp"),
            P("grp"),
            P(None, ("cell", "grp"), None),
            P(None, ("cell", "grp"), None),
            P(("cell", "grp"), None),
            P(("cell", "grp"), None),
            P(("cell", "grp")),
        ),
        out_specs=(P(None, "grp"), P(None, ("cell", "grp"), None)),
        check_vma=False,
    )
```

```python
import functools

import jax
import jax.numpy as jnp
from jax import lax
from jax.experimental import pallas as pl
from jax.experimental.pallas import tpu as pltpu
from jax.sharding import PartitionSpec as P

RIM = 2048
ITERS = 3
LANES = 128

relax_factor = 0.6
tangent_floor = 0.05


def split_terms(value):
    high = value.astype(jnp.bfloat16)
    low = (value - high.astype(jnp.float32)).astype(jnp.bfloat16)
    return high, low


def kernel(
    cells,
    counts_ref, v_ref, mass_ref, pairs_ref, angles_ref, bias_ref, friction_ref,
    vel_out, imp_out,
    hot1, hot2, row1, row2, active,
    h1_ref, h2_ref, l1_ref, l2_ref,
    vb, vfree_all, mass_all, rel, partial, force_ref, acc_outer, acc_inner,
    edge_out, edge_in, outer, outer_in, inner, inner_in, bound_out, bound_in,
    edge_send, edge_recv, outer_send, outer_recv, inner_send, inner_recv, bound_send, bound_recv,
):
    rows = v_ref.shape[1]
    rim = RIM // LANES
    half = rows // 2
    deep = half + rim
    mid = half - rim
    tiles = pairs_ref.shape[1] // 8
    core = lax.axis_index("cell")
    cell = lax.axis_index("grp")
    has_prev = cell > 0
    has_next = cell < cells - 1
    present = (has_prev, has_next)
    steps = (-1, 1)

    barrier = pltpu.get_barrier_semaphore()
    pl.semaphore_signal(barrier, inc=1, device_id={"cell": 1 - core}, device_id_type=pl.DeviceIdType.MESH)
    for side in range(2):
        @pl.when(present[side])
        def _():
            pl.semaphore_signal(
                barrier, inc=1, device_id={"grp": cell + steps[side]}, device_id_type=pl.DeviceIdType.MESH
            )

    edge_out[0, 0:3] = v_ref[:, 0:rim]
    edge_out[0, 3] = mass_ref[0:rim]
    edge_out[1, 0:3] = v_ref[:, rows - rim:rows]
    edge_out[1, 3] = mass_ref[rows - rim:rows]
    for side in range(2):
        @pl.when(jnp.logical_not(present[side]))
        def _():
            edge_in[side] = jnp.zeros(edge_in.shape[1:], jnp.float32)
            for sweep in range(ITERS):
                bound_in[sweep, side] = jnp.zeros(bound_in.shape[2:], jnp.float32)

    between = jnp.logical_and(has_prev, has_next)

    @pl.when(between)
    def _():
        pl.semaphore_wait(barrier, 3)

    @pl.when(jnp.logical_not(between))
    def _():
        pl.semaphore_wait(barrier, 2)

    def edge_copy(side):
        return pltpu.make_async_remote_copy(
            src_ref=edge_out.at[side], dst_ref=edge_in.at[1 - side],
            send_sem=edge_send.at[side], recv_sem=edge_recv.at[1 - side],
            device_id={"grp": cell + steps[side]}, device_id_type=pl.DeviceIdType.MESH,
        )

    def outer_copy(sweep):
        return pltpu.make_async_remote_copy(
            src_ref=outer.at[sweep], dst_ref=outer_in.at[sweep],
            send_sem=outer_send.at[sweep], recv_sem=outer_recv.at[sweep],
            device_id={"cell": 1 - core}, device_id_type=pl.DeviceIdType.MESH,
        )

    def inner_copy(sweep):
        return pltpu.make_async_remote_copy(
            src_ref=inner.at[sweep], dst_ref=inner_in.at[sweep],
            send_sem=inner_send.at[sweep], recv_sem=inner_recv.at[sweep],
            device_id={"cell": 1 - core}, device_id_type=pl.DeviceIdType.MESH,
        )

    def bound_copy(sweep, side):
        size = rim if sweep == ITERS - 1 else 2 * rim
        return pltpu.make_async_remote_copy(
            src_ref=bound_out.at[sweep, side, :, pl.ds(0, size)],
            dst_ref=bound_in.at[sweep, 1 - side, :, pl.ds(0, size)],
            send_sem=bound_send.at[sweep, side], recv_sem=bound_recv.at[sweep, 1 - side],
            device_id={"grp": cell + steps[side]}, device_id_type=pl.DeviceIdType.MESH,
        )

    for side in range(2):
        @pl.when(present[side])
        def _():
            edge_copy(side).start()

    def place(position):
        own = position - RIM
        r = own >> 7
        lane = own & (LANES - 1)
        upper = r >= half
        h = jnp.where(upper, jnp.where(r >= rows - rim, r - (rows - rim), r - (half - rim)), r)
        l = jnp.where(upper, LANES, 0) + lane
        before = position < RIM
        after = own >= rows * LANES
        h = jnp.where(before, half + (position >> 7), jnp.where(after, half + r - rows, h))
        l = jnp.where(before, lane, jnp.where(after, LANES + lane, l))
        return h, l

    h1_ref[...], l1_ref[...] = place(pairs_ref[0])
    h2_ref[...], l2_ref[...] = place(pairs_ref[1])

    slot = lax.broadcasted_iota(jnp.int32, (1, LANES), 1)
    for r in range(pairs_ref.shape[1]):
        active[r:r + 1, :] = jnp.where(slot < counts_ref[r], 1.0, 0.0)

    def pair_row(tile, u):
        return jnp.concatenate([tile[2 * u:2 * u + 1], tile[2 * u + 1:2 * u + 2]], axis=1)

    wide = 2 * LANES
    iota_l = lax.broadcasted_iota(jnp.int32, (wide, wide), 0)
    iota_h = lax.broadcasted_iota(jnp.int32, (half, wide), 0)
    iota_o = lax.broadcasted_iota(jnp.int32, (rim, wide), 0)
    iota_m = lax.broadcasted_iota(jnp.int32, (mid, wide), 0) + rim
    iota_r = lax.broadcasted_iota(jnp.int32, (rim, wide), 0) + half

    sin_p, cos_p = jnp.sin(angles_ref[0]), jnp.cos(angles_ref[0])
    sin_q, cos_q = jnp.sin(angles_ref[1]), jnp.cos(angles_ref[1])
    normal = (sin_p * cos_q, sin_p * sin_q, cos_p)
    first_tan = (cos_p * cos_q, cos_p * sin_q, -sin_p)
    second_tan = (-sin_q, cos_q)

    def fold(block):
        lower = block[..., 0:half, :]
        upper = jnp.concatenate([block[..., rows - rim:rows, :], block[..., half:rows - rim, :]], axis=-2)
        return jnp.concatenate([lower, upper], axis=-1)

    vfree_all[:, 0:half] = fold(v_ref[...])
    mass_all[0:half] = fold(mass_ref[...])

    def tile_at(i):
        return pl.ds(pl.multiple_of(i * 8, 8), 8)

    def store_terms(parts, base):
        count, size = len(parts), parts[0].shape[0]
        for c, part in enumerate(parts):
            for t, term in enumerate(split_terms(part)):
                at = base + (t * count + c) * size
                vb[at:at + size, :] = term

    def picked(g, base, size, c, count, mask):
        a = base + c * size
        b = a + count * size
        block = jnp.where(mask, g[a:a + size] + g[b:b + size], 0.0)
        return jnp.sum(block.reshape(size // 8, 8, wide), axis=0)

    def gather_inner(count, fresh):
        @pl.loop(0, tiles)
        def _(i):
            h1, h2 = h1_ref[tile_at(i), :], h2_ref[tile_at(i), :]
            l1, l2 = l1_ref[tile_at(i), :], l2_ref[tile_at(i), :]
            for u in range(4):
                cut = slice(u * wide, (u + 1) * wide)
                h1_row, h2_row = pair_row(h1, u), pair_row(h2, u)
                if fresh:
                    hot1[i, :, cut] = jnp.where(iota_l == pair_row(l1, u), 1.0, 0.0).astype(jnp.bfloat16)
                    hot2[i, :, cut] = jnp.where(iota_l == pair_row(l2, u), 1.0, 0.0).astype(jnp.bfloat16)
                    row1[i, :, cut] = jnp.where(iota_h == h1_row, 1.0, 0.0).astype(jnp.bfloat16)
                    row2[i, 0:half, cut] = jnp.where(iota_h == h2_row, 1.0, 0.0).astype(jnp.bfloat16)
                    row2[i, half:deep, cut] = jnp.where(iota_r == h2_row, 1.0, 0.0).astype(jnp.bfloat16)
                source = vb[0:2 * count * mid, :]
                g1 = jnp.dot(source, hot1[i, :, cut], preferred_element_type=jnp.float32)
                g2 = jnp.dot(source, hot2[i, :, cut], preferred_element_type=jnp.float32)
                at1, at2 = iota_m == h1_row, iota_m == h2_row
                for c in range(count):
                    first = picked(g1, 0, mid, c, count, at1)
                    second = picked(g2, 0, mid, c, count, at2)
                    partial[i, u, c] = first + second if c == 3 else first - second

    def gather_outer(count):
        base = 2 * count * mid
        own = 2 * count * rim

        @pl.loop(0, tiles)
        def _(i):
            h1, h2 = h1_ref[tile_at(i), :], h2_ref[tile_at(i), :]
            found = [[] for _ in range(count)]
            for u in range(4):
                cut = slice(u * wide, (u + 1) * wide)
                h1_row, h2_row = pair_row(h1, u), pair_row(h2, u)
                g1 = jnp.dot(vb[base:base + own, :], hot1[i, :, cut], preferred_element_type=jnp.float32)
                g2 = jnp.dot(vb[base:base + 2 * own, :], hot2[i, :, cut], preferred_element_type=jnp.float32)
                at1, at2, at_rim = iota_o == h1_row, iota_o == h2_row, iota_r == h2_row
                for c in range(count):
                    first = picked(g1, 0, rim, c, count, at1)
                    second = picked(g2, 0, rim, c, count, at2) + picked(g2, own, rim, c, count, at_rim)
                    both_ends = partial[i, u, c] + (first + second if c == 3 else first - second)
                    line = jnp.sum(both_ends, axis=0, keepdims=True)
                    found[c] += [line[:, 0:LANES], line[:, LANES:wide]]
            for c in range(count):
                rel[c, tile_at(i), :] = jnp.concatenate(found[c], axis=0)

    contract = (((1,), (1,)), ((), ()))

    def force_terms(i):
        pieces = []
        for c in range(3):
            tile = force_ref[c, tile_at(i), :]
            wide_row = jnp.concatenate([tile[s:s + 1] for s in range(8)], axis=1)
            pieces.append(split_terms(jnp.broadcast_to(wide_row, (16, 8 * LANES))))
        return pieces

    def weigh(mask, pieces, sign):
        size = mask.shape[0]
        done = []
        for t in range(2):
            for c in range(3):
                block = mask.reshape(size // 16, 16, 8 * LANES) * (sign * pieces[c][t])[None]
                done.append(block.reshape(size, 8 * LANES))
        return done

    def product(weighed, hot):
        return lax.dot_general(
            jnp.concatenate(weighed, axis=0), hot, contract, preferred_element_type=jnp.float32
        )

    def scatter_outer():
        acc_outer[...] = jnp.zeros(acc_outer.shape, jnp.float32)

        @pl.loop(0, tiles)
        def _(i):
            pieces = force_terms(i)
            mine = weigh(row1[i, 0:rim], pieces, 1)
            theirs = weigh(row2[i, 0:rim], pieces, -1) + weigh(row2[i, half:deep], pieces, -1)
            acc_outer[0:6 * rim, :] += product(mine, hot1[i])
            acc_outer[...] += product(theirs, hot2[i])

    def scatter_inner(begin, end):
        @pl.loop(begin, end)
        def _(i):
            pieces = force_terms(i)
            mine = product(weigh(row1[i, rim:half], pieces, 1), hot1[i])
            theirs = product(weigh(row2[i, rim:half], pieces, -1), hot2[i])
            acc_inner[...] += mine + theirs

    lambdas = [jnp.zeros(bias_ref.shape, jnp.float32)] * 3
    reduced = None
    for sweep in range(ITERS):
        last = sweep == ITERS - 1
        if sweep == 0:
            store_terms([vfree_all[c, rim:half] for c in range(3)] + [mass_all[rim:half]], 0)
            gather_inner(4, True)
            for side in range(2):
                @pl.when(present[side])
                def _():
                    edge_copy(1 - side).wait_recv()
            for side in range(2):
                cut = slice(side * LANES, (side + 1) * LANES)
                vfree_all[:, half:deep, cut] = edge_in[side, 0:3]
                mass_all[half:deep, cut] = edge_in[side, 3]
            base = 8 * mid
            store_terms([vfree_all[c, 0:rim] for c in range(3)] + [mass_all[0:rim]], base)
            store_terms([vfree_all[c, half:deep] for c in range(3)] + [mass_all[half:deep]], base + 8 * rim)
            gather_outer(4)
            reduced = relax_factor / rel[3]
        x, y, z = rel[0], rel[1], rel[2]
        speed_n = normal[0] * x + normal[1] * y + normal[2] * z + bias_ref[...]
        speed_a = first_tan[0] * x + first_tan[1] * y + first_tan[2] * z
        speed_b = second_tan[0] * x + second_tan[1] * y
        trial_n = lambdas[0] - reduced * speed_n
        trial_a = lambdas[1] - reduced * speed_a
        trial_b = lambdas[2] - reduced * speed_b
        normal_imp = jnp.maximum(trial_n, 0.0)
        tan_size = jnp.sqrt(trial_a * trial_a + trial_b * trial_b)
        factor = jnp.minimum(1.0, friction_ref[...] * normal_imp / jnp.maximum(tan_size, tangent_floor))
        live = active[...]
        lambdas = [normal_imp * live, trial_a * factor * live, trial_b * factor * live]
        for c in range(3):
            force = normal[c] * lambdas[0] + first_tan[c] * lambdas[1]
            if c < 2:
                force = force + second_tan[c] * lambdas[2]
            force_ref[c] = force

        scatter_outer()
        for c in range(3):
            for part in range(2):
                a = (6 * part + c) * rim
                b = a + 3 * rim
                outer[sweep, c, part * rim:(part + 1) * rim] = acc_outer[a:a + rim, :] + acc_outer[b:b + rim, :]
        outer_copy(sweep).start()
        acc_inner[...] = jnp.zeros(acc_inner.shape, jnp.float32)
        scatter_inner(0, tiles // 2)
        outer_copy(sweep).wait_recv()
        for side in range(2):
            cut = slice(side * LANES, (side + 1) * LANES)
            bound_out[sweep, side, :, 0:rim] = outer[sweep, :, rim:2 * rim, cut] + outer_in[sweep, :, rim:2 * rim, cut]
            bound_out[sweep, side, :, rim:2 * rim] = outer[sweep, :, 0:rim, cut] + outer_in[sweep, :, 0:rim, cut]
        for side in range(2):
            @pl.when(present[side])
            def _():
                bound_copy(sweep, side).start()
        scatter_inner(tiles // 2, tiles)
        for c in range(3):
            a = c * mid
            b = a + 3 * mid
            inner[sweep, c] = acc_inner[a:a + mid, :] + acc_inner[b:b + mid, :]
        inner_copy(sweep).start()
        inner_copy(sweep).wait_recv()
        speeds = []
        for c in range(3):
            total = inner[sweep, c] + inner_in[sweep, c]
            speeds.append(vfree_all[c, rim:half] + mass_all[rim:half] * total)
        if last:
            for c in range(3):
                vel_out[c, rim:half] = speeds[c][:, 0:LANES]
                vel_out[c, half:rows - rim] = speeds[c][:, LANES:wide]
                imp_out[c] = lambdas[c]
        else:
            store_terms(speeds, 0)
            gather_inner(3, False)
        for side in range(2):
            @pl.when(present[side])
            def _():
                bound_copy(sweep, 1 - side).wait_recv()
        for part in range(1 if last else 2):
            here = slice((1 - part) * rim, (2 - part) * rim)
            there = slice(part * rim, (part + 1) * rim)
            body = slice(0, rim) if part == 0 else slice(half, deep)
            speeds = []
            for c in range(3):
                total = jnp.concatenate(
                    [bound_out[sweep, s, c, here] + bound_in[sweep, s, c, there] for s in range(2)], axis=-1
                )
                speeds.append(vfree_all[c, body] + mass_all[body] * total)
            if last:
                for c in range(3):
                    vel_out[c, 0:rim] = speeds[c][:, 0:LANES]
                    vel_out[c, rows - rim:rows] = speeds[c][:, LANES:wide]
            else:
                store_terms(speeds, 6 * mid + 6 * rim * part)
        if not last:
            gather_outer(3)
    for side in range(2):
        @pl.when(present[side])
        def _():
            edge_copy(side).wait_send()
            for sweep in range(ITERS):
                bound_copy(sweep, side).wait_send()
    for sweep in range(ITERS):
        outer_copy(sweep).wait_send()
        inner_copy(sweep).wait_send()


def on_device(cells, v_free, inv_mass, pairs, angles, bias, friction, counts):
    width = v_free.shape[1]
    blocks, slots = bias.shape
    rows = width // LANES
    rim = RIM // LANES
    half = rows // 2
    deep = half + rim
    mid = half - rim
    tiles = blocks // 8
    wide = 2 * LANES
    f32, bf16, i32 = jnp.float32, jnp.bfloat16, jnp.int32
    vmem = pl.BlockSpec(memory_space=pltpu.VMEM)
    dma = pltpu.SemaphoreType.DMA
    velocity, impulses = pl.pallas_call(
        functools.partial(kernel, cells),
        out_shape=(
            jax.ShapeDtypeStruct((3, rows, LANES), f32),
            jax.ShapeDtypeStruct((3, blocks, slots), f32),
        ),
        in_specs=[pl.BlockSpec(memory_space=pltpu.SMEM)] + [vmem] * 6,
        out_specs=(vmem, vmem),
        scratch_shapes=[
            pltpu.VMEM((tiles, wide, 8 * LANES), bf16),
            pltpu.VMEM((tiles, wide, 8 * LANES), bf16),
            pltpu.VMEM((tiles, half, 8 * LANES), bf16),
            pltpu.VMEM((tiles, deep, 8 * LANES), bf16),
            pltpu.VMEM((blocks, slots), f32),
            pltpu.VMEM((blocks, slots), i32),
            pltpu.VMEM((blocks, slots), i32),
            pltpu.VMEM((blocks, slots), i32),
            pltpu.VMEM((blocks, slots), i32),
            pltpu.VMEM((8 * deep, wide), bf16),
            pltpu.VMEM((3, deep, wide), f32),
            pltpu.VMEM((deep, wide), f32),
            pltpu.VMEM((4, blocks, slots), f32),
            pltpu.VMEM((tiles, 4, 4, 8, wide), f32),
            pltpu.VMEM((3, blocks, slots), f32),
            pltpu.VMEM((12 * rim, wide), f32),
            pltpu.VMEM((6 * mid, wide), f32),
            pltpu.VMEM((2, 4, rim, LANES), f32),
            pltpu.VMEM((2, 4, rim, LANES), f32),
            pltpu.VMEM((ITERS, 3, 2 * rim, wide), f32),
            pltpu.VMEM((ITERS, 3, 2 * rim, wide), f32),
            pltpu.VMEM((ITERS, 3, mid, wide), f32),
            pltpu.VMEM((ITERS, 3, mid, wide), f32),
            pltpu.VMEM((ITERS, 2, 3, 2 * rim, LANES), f32),
            pltpu.VMEM((ITERS, 2, 3, 2 * rim, LANES), f32),
            dma((2,)),
            dma((2,)),
            dma((ITERS,)),
            dma((ITERS,)),
            dma((ITERS,)),
            dma((ITERS,)),
            dma((ITERS, 2)),
            dma((ITERS, 2)),
        ],
        compiler_params=pltpu.CompilerParams(
            collective_id=0, has_side_effects=True, vmem_limit_bytes=40 * 1024 * 1024
        ),
    )(
        counts,
        v_free.reshape(3, rows, LANES),
        inv_mass.reshape(rows, LANES),
        pairs, angles, bias, friction,
    )
    return velocity.reshape(3, width), impulses


def solution(mesh):
    return jax.shard_map(
        functools.partial(on_device, mesh.shape["grp"]),
        mesh=mesh,
        in_specs=(
            P(None, "grp"),
            P("grp"),
            P(None, ("cell", "grp"), None),
            P(None, ("cell", "grp"), None),
            P(("cell", "grp"), None),
            P(("cell", "grp"), None),
            P(("cell", "grp")),
        ),
        out_specs=(P(None, "grp"), P(None, ("cell", "grp"), None)),
        check_vma=False,
    )
```

```python
import functools

import jax
import jax.numpy as jnp
from jax import lax
from jax.experimental import pallas as pl
from jax.experimental.pallas import tpu as pltpu
from jax.sharding import PartitionSpec as P

RIM = 2048
ITERS = 3
LANES = 128

relax_factor = 0.6
tangent_floor = 0.05


def split_terms(value):
    high = value.astype(jnp.bfloat16)
    low = (value - high.astype(jnp.float32)).astype(jnp.bfloat16)
    return high, low


def kernel(
    cells,
    counts_ref, v_ref, mass_ref, pairs_ref, angles_ref, bias_ref, friction_ref,
    vel_out, imp_out,
    hot1, hot2, spot1, spot2, row1, row2, active,
    h1_ref, h2_ref, l1_ref, l2_ref,
    vb, vfree_all, mass_all, rel, partial, force_ref, acc_outer, acc_inner,
    edge_out, edge_in, outer, outer_in, inner, inner_in, bound_out, bound_in,
    edge_send, edge_recv, outer_send, outer_recv, inner_send, inner_recv, bound_send, bound_recv,
):
    rows = v_ref.shape[1]
    rim = RIM // LANES
    half = rows // 2
    deep = half + rim
    mid = half - rim
    tiles = pairs_ref.shape[1] // 8
    core = lax.axis_index("cell")
    cell = lax.axis_index("grp")
    has_prev = cell > 0
    has_next = cell < cells - 1
    present = (has_prev, has_next)
    steps = (-1, 1)

    barrier = pltpu.get_barrier_semaphore()
    pl.semaphore_signal(barrier, inc=1, device_id={"cell": 1 - core}, device_id_type=pl.DeviceIdType.MESH)
    for side in range(2):
        @pl.when(present[side])
        def _():
            pl.semaphore_signal(
                barrier, inc=1, device_id={"grp": cell + steps[side]}, device_id_type=pl.DeviceIdType.MESH
            )

    edge_out[0, 0:3] = v_ref[:, 0:rim]
    edge_out[0, 3] = mass_ref[0:rim]
    edge_out[1, 0:3] = v_ref[:, rows - rim:rows]
    edge_out[1, 3] = mass_ref[rows - rim:rows]
    for side in range(2):
        @pl.when(jnp.logical_not(present[side]))
        def _():
            edge_in[side] = jnp.zeros(edge_in.shape[1:], jnp.float32)
            for sweep in range(ITERS):
                bound_in[sweep, side] = jnp.zeros(bound_in.shape[2:], jnp.float32)

    between = jnp.logical_and(has_prev, has_next)

    @pl.when(between)
    def _():
        pl.semaphore_wait(barrier, 3)

    @pl.when(jnp.logical_not(between))
    def _():
        pl.semaphore_wait(barrier, 2)

    def edge_copy(side):
        return pltpu.make_async_remote_copy(
            src_ref=edge_out.at[side], dst_ref=edge_in.at[1 - side],
            send_sem=edge_send.at[side], recv_sem=edge_recv.at[1 - side],
            device_id={"grp": cell + steps[side]}, device_id_type=pl.DeviceIdType.MESH,
        )

    def outer_copy(sweep):
        return pltpu.make_async_remote_copy(
            src_ref=outer.at[sweep], dst_ref=outer_in.at[sweep],
            send_sem=outer_send.at[sweep], recv_sem=outer_recv.at[sweep],
            device_id={"cell": 1 - core}, device_id_type=pl.DeviceIdType.MESH,
        )

    def inner_copy(sweep):
        return pltpu.make_async_remote_copy(
            src_ref=inner.at[sweep], dst_ref=inner_in.at[sweep],
            send_sem=inner_send.at[sweep], recv_sem=inner_recv.at[sweep],
            device_id={"cell": 1 - core}, device_id_type=pl.DeviceIdType.MESH,
        )

    def bound_copy(sweep, side):
        size = rim if sweep == ITERS - 1 else 2 * rim
        return pltpu.make_async_remote_copy(
            src_ref=bound_out.at[sweep, side, :, pl.ds(0, size)],
            dst_ref=bound_in.at[sweep, 1 - side, :, pl.ds(0, size)],
            send_sem=bound_send.at[sweep, side], recv_sem=bound_recv.at[sweep, 1 - side],
            device_id={"grp": cell + steps[side]}, device_id_type=pl.DeviceIdType.MESH,
        )

    for side in range(2):
        @pl.when(present[side])
        def _():
            edge_copy(side).start()

    def place(position):
        own = position - RIM
        r = own >> 7
        lane = own & (LANES - 1)
        upper = r >= half
        h = jnp.where(upper, jnp.where(r >= rows - rim, r - (rows - rim), r - (half - rim)), r)
        l = jnp.where(upper, LANES, 0) + lane
        before = position < RIM
        after = own >= rows * LANES
        h = jnp.where(before, half + (position >> 7), jnp.where(after, half + r - rows, h))
        l = jnp.where(before, lane, jnp.where(after, LANES + lane, l))
        return h, l

    h1_ref[...], l1_ref[...] = place(pairs_ref[0])
    h2_ref[...], l2_ref[...] = place(pairs_ref[1])

    slot = lax.broadcasted_iota(jnp.int32, (1, LANES), 1)
    for r in range(pairs_ref.shape[1]):
        active[r:r + 1, :] = jnp.where(slot < counts_ref[r], 1.0, 0.0)

    def pair_row(tile, u):
        return jnp.concatenate([tile[2 * u:2 * u + 1], tile[2 * u + 1:2 * u + 2]], axis=1)

    wide = 2 * LANES
    iota_l = lax.broadcasted_iota(jnp.int32, (wide, wide), 0)
    iota_h = lax.broadcasted_iota(jnp.int32, (half, wide), 0)
    iota_c = lax.broadcasted_iota(jnp.int32, (LANES, LANES), 1).astype(jnp.float32)
    iota_o = lax.broadcasted_iota(jnp.int32, (rim, wide), 0)
    iota_m = lax.broadcasted_iota(jnp.int32, (mid, wide), 0) + rim
    iota_r = lax.broadcasted_iota(jnp.int32, (rim, wide), 0) + half

    sin_p, cos_p = jnp.sin(angles_ref[0]), jnp.cos(angles_ref[0])
    sin_q, cos_q = jnp.sin(angles_ref[1]), jnp.cos(angles_ref[1])
    normal = (sin_p * cos_q, sin_p * sin_q, cos_p)
    first_tan = (cos_p * cos_q, cos_p * sin_q, -sin_p)
    second_tan = (-sin_q, cos_q)

    def fold(block):
        lower = block[..., 0:half, :]
        upper = jnp.concatenate([block[..., rows - rim:rows, :], block[..., half:rows - rim, :]], axis=-2)
        return jnp.concatenate([lower, upper], axis=-1)

    vfree_all[:, 0:half] = fold(v_ref[...])
    mass_all[0:half] = fold(mass_ref[...])

    def tile_at(i):
        return pl.ds(pl.multiple_of(i * 8, 8), 8)

    def store_terms(parts, base):
        count, size = len(parts), parts[0].shape[0]
        for c, part in enumerate(parts):
            for t, term in enumerate(split_terms(part)):
                at = base + (t * count + c) * size
                vb[at:at + size, :] = term

    def picked(g, base, size, c, count, mask):
        a = base + c * size
        b = a + count * size
        block = jnp.where(mask, g[a:a + size] + g[b:b + size], 0.0)
        return jnp.sum(block.reshape(size // 8, 8, wide), axis=0)

    def gather_inner(count, fresh):
        @pl.loop(0, tiles)
        def _(i):
            h1, h2 = h1_ref[tile_at(i), :], h2_ref[tile_at(i), :]
            l1, l2 = l1_ref[tile_at(i), :], l2_ref[tile_at(i), :]
            for u in range(4):
                cut = slice(u * wide, (u + 1) * wide)
                h1_row, h2_row = pair_row(h1, u), pair_row(h2, u)
                if fresh:
                    hot1[i, :, cut] = jnp.where(iota_l == pair_row(l1, u), 1.0, 0.0).astype(jnp.bfloat16)
                    hot2[i, :, cut] = jnp.where(iota_l == pair_row(l2, u), 1.0, 0.0).astype(jnp.bfloat16)
                    for spot, l in ((spot1, l1), (spot2, l2)):
                        for s in (2 * u, 2 * u + 1):
                            lane_row = l[s:s + 1].astype(jnp.float32)
                            column = jnp.broadcast_to(lane_row, (LANES, LANES)).T
                            for side in range(2):
                                found_at = jnp.where(column == iota_c + (side * LANES), 1.0, 0.0)
                                spot[i, s * LANES:(s + 1) * LANES, side * LANES:(side + 1) * LANES] = (
                                    found_at.astype(jnp.bfloat16)
                                )
                    row1[i, :, cut] = jnp.where(iota_h == h1_row, 1.0, 0.0).astype(jnp.bfloat16)
                    row2[i, 0:half, cut] = jnp.where(iota_h == h2_row, 1.0, 0.0).astype(jnp.bfloat16)
                    row2[i, half:deep, cut] = jnp.where(iota_r == h2_row, 1.0, 0.0).astype(jnp.bfloat16)
                source = vb[0:2 * count * mid, :]
                g1 = jnp.dot(source, hot1[i, :, cut], preferred_element_type=jnp.float32)
                g2 = jnp.dot(source, hot2[i, :, cut], preferred_element_type=jnp.float32)
                at1, at2 = iota_m == h1_row, iota_m == h2_row
                for c in range(count):
                    first = picked(g1, 0, mid, c, count, at1)
                    second = picked(g2, 0, mid, c, count, at2)
                    partial[i, u, c] = first + second if c == 3 else first - second

    def gather_outer(count):
        base = 2 * count * mid
        own = 2 * count * rim

        @pl.loop(0, tiles)
        def _(i):
            h1, h2 = h1_ref[tile_at(i), :], h2_ref[tile_at(i), :]
            found = [[] for _ in range(count)]
            for u in range(4):
                cut = slice(u * wide, (u + 1) * wide)
                h1_row, h2_row = pair_row(h1, u), pair_row(h2, u)
                g1 = jnp.dot(vb[base:base + own, :], hot1[i, :, cut], preferred_element_type=jnp.float32)
                g2 = jnp.dot(vb[base:base + 2 * own, :], hot2[i, :, cut], preferred_element_type=jnp.float32)
                at1, at2, at_rim = iota_o == h1_row, iota_o == h2_row, iota_r == h2_row
                for c in range(count):
                    first = picked(g1, 0, rim, c, count, at1)
                    second = picked(g2, 0, rim, c, count, at2) + picked(g2, own, rim, c, count, at_rim)
                    both_ends = partial[i, u, c] + (first + second if c == 3 else first - second)
                    line = jnp.sum(both_ends, axis=0, keepdims=True)
                    found[c] += [line[:, 0:LANES], line[:, LANES:wide]]
            for c in range(count):
                rel[c, tile_at(i), :] = jnp.concatenate(found[c], axis=0)

    def force_terms(i):
        pieces = []
        for c in range(3):
            tile = force_ref[c, tile_at(i), :]
            wide_row = jnp.concatenate([tile[s:s + 1] for s in range(8)], axis=1)
            pieces.append(split_terms(jnp.broadcast_to(wide_row, (16, 8 * LANES))))
        return pieces

    def weigh(mask, pieces, sign):
        size = mask.shape[0]
        done = []
        for t in range(2):
            for c in range(3):
                block = mask.reshape(size // 16, 16, 8 * LANES) * (sign * pieces[c][t])[None]
                done.append(block.reshape(size, 8 * LANES))
        return done

    def product(weighed, hot):
        return jnp.dot(jnp.concatenate(weighed, axis=0), hot, preferred_element_type=jnp.float32)

    def scatter_outer():
        acc_outer[...] = jnp.zeros(acc_outer.shape, jnp.float32)

        @pl.loop(0, tiles)
        def _(i):
            pieces = force_terms(i)
            mine = weigh(row1[i, 0:rim], pieces, 1)
            theirs = weigh(row2[i, 0:rim], pieces, -1) + weigh(row2[i, half:deep], pieces, -1)
            acc_outer[0:6 * rim, :] += product(mine, spot1[i])
            acc_outer[...] += product(theirs, spot2[i])

    def scatter_inner(begin, end):
        @pl.loop(begin, end)
        def _(i):
            pieces = force_terms(i)
            mine = product(weigh(row1[i, rim:half], pieces, 1), spot1[i])
            theirs = product(weigh(row2[i, rim:half], pieces, -1), spot2[i])
            acc_inner[...] += mine + theirs

    lambdas = [jnp.zeros(bias_ref.shape, jnp.float32)] * 3
    reduced = None
    for sweep in range(ITERS):
        last = sweep == ITERS - 1
        if sweep == 0:
            store_terms([vfree_all[c, rim:half] for c in range(3)] + [mass_all[rim:half]], 0)
            gather_inner(4, True)
            for side in range(2):
                @pl.when(present[side])
                def _():
                    edge_copy(1 - side).wait_recv()
            for side in range(2):
                cut = slice(side * LANES, (side + 1) * LANES)
                vfree_all[:, half:deep, cut] = edge_in[side, 0:3]
                mass_all[half:deep, cut] = edge_in[side, 3]
            base = 8 * mid
            store_terms([vfree_all[c, 0:rim] for c in range(3)] + [mass_all[0:rim]], base)
            store_terms([vfree_all[c, half:deep] for c in range(3)] + [mass_all[half:deep]], base + 8 * rim)
            gather_outer(4)
            reduced = relax_factor / rel[3]
        x, y, z = rel[0], rel[1], rel[2]
        speed_n = normal[0] * x + normal[1] * y + normal[2] * z + bias_ref[...]
        speed_a = first_tan[0] * x + first_tan[1] * y + first_tan[2] * z
        speed_b = second_tan[0] * x + second_tan[1] * y
        trial_n = lambdas[0] - reduced * speed_n
        trial_a = lambdas[1] - reduced * speed_a
        trial_b = lambdas[2] - reduced * speed_b
        normal_imp = jnp.maximum(trial_n, 0.0)
        tan_size = jnp.sqrt(trial_a * trial_a + trial_b * trial_b)
        factor = jnp.minimum(1.0, friction_ref[...] * normal_imp / jnp.maximum(tan_size, tangent_floor))
        live = active[...]
        lambdas = [normal_imp * live, trial_a * factor * live, trial_b * factor * live]
        for c in range(3):
            force = normal[c] * lambdas[0] + first_tan[c] * lambdas[1]
            if c < 2:
                force = force + second_tan[c] * lambdas[2]
            force_ref[c] = force

        scatter_outer()
        for c in range(3):
            for part in range(2):
                a = (6 * part + c) * rim
                b = a + 3 * rim
                outer[sweep, c, part * rim:(part + 1) * rim] = acc_outer[a:a + rim, :] + acc_outer[b:b + rim, :]
        outer_copy(sweep).start()
        acc_inner[...] = jnp.zeros(acc_inner.shape, jnp.float32)
        scatter_inner(0, tiles // 2)
        outer_copy(sweep).wait_recv()
        for side in range(2):
            cut = slice(side * LANES, (side + 1) * LANES)
            bound_out[sweep, side, :, 0:rim] = outer[sweep, :, rim:2 * rim, cut] + outer_in[sweep, :, rim:2 * rim, cut]
            bound_out[sweep, side, :, rim:2 * rim] = outer[sweep, :, 0:rim, cut] + outer_in[sweep, :, 0:rim, cut]
        for side in range(2):
            @pl.when(present[side])
            def _():
                bound_copy(sweep, side).start()
        scatter_inner(tiles // 2, tiles)
        for c in range(3):
            a = c * mid
            b = a + 3 * mid
            inner[sweep, c] = acc_inner[a:a + mid, :] + acc_inner[b:b + mid, :]
        inner_copy(sweep).start()
        inner_copy(sweep).wait_recv()
        speeds = []
        for c in range(3):
            total = inner[sweep, c] + inner_in[sweep, c]
            speeds.append(vfree_all[c, rim:half] + mass_all[rim:half] * total)
        if last:
            for c in range(3):
                vel_out[c, rim:half] = speeds[c][:, 0:LANES]
                vel_out[c, half:rows - rim] = speeds[c][:, LANES:wide]
                imp_out[c] = lambdas[c]
        else:
            store_terms(speeds, 0)
            gather_inner(3, False)
        for side in range(2):
            @pl.when(present[side])
            def _():
                bound_copy(sweep, 1 - side).wait_recv()
        for part in range(1 if last else 2):
            here = slice((1 - part) * rim, (2 - part) * rim)
            there = slice(part * rim, (part + 1) * rim)
            body = slice(0, rim) if part == 0 else slice(half, deep)
            speeds = []
            for c in range(3):
                total = jnp.concatenate(
                    [bound_out[sweep, s, c, here] + bound_in[sweep, s, c, there] for s in range(2)], axis=-1
                )
                speeds.append(vfree_all[c, body] + mass_all[body] * total)
            if last:
                for c in range(3):
                    vel_out[c, 0:rim] = speeds[c][:, 0:LANES]
                    vel_out[c, rows - rim:rows] = speeds[c][:, LANES:wide]
            else:
                store_terms(speeds, 6 * mid + 6 * rim * part)
        if not last:
            gather_outer(3)
    for side in range(2):
        @pl.when(present[side])
        def _():
            edge_copy(side).wait_send()
            for sweep in range(ITERS):
                bound_copy(sweep, side).wait_send()
    for sweep in range(ITERS):
        outer_copy(sweep).wait_send()
        inner_copy(sweep).wait_send()


def on_device(cells, v_free, inv_mass, pairs, angles, bias, friction, counts):
    width = v_free.shape[1]
    blocks, slots = bias.shape
    rows = width // LANES
    rim = RIM // LANES
    half = rows // 2
    deep = half + rim
    mid = half - rim
    tiles = blocks // 8
    wide = 2 * LANES
    f32, bf16, i32 = jnp.float32, jnp.bfloat16, jnp.int32
    vmem = pl.BlockSpec(memory_space=pltpu.VMEM)
    dma = pltpu.SemaphoreType.DMA
    velocity, impulses = pl.pallas_call(
        functools.partial(kernel, cells),
        out_shape=(
            jax.ShapeDtypeStruct((3, rows, LANES), f32),
            jax.ShapeDtypeStruct((3, blocks, slots), f32),
        ),
        in_specs=[pl.BlockSpec(memory_space=pltpu.SMEM)] + [vmem] * 6,
        out_specs=(vmem, vmem),
        scratch_shapes=[
            pltpu.VMEM((tiles, wide, 8 * LANES), bf16),
            pltpu.VMEM((tiles, wide, 8 * LANES), bf16),
            pltpu.VMEM((tiles, 8 * LANES, wide), bf16),
            pltpu.VMEM((tiles, 8 * LANES, wide), bf16),
            pltpu.VMEM((tiles, half, 8 * LANES), bf16),
            pltpu.VMEM((tiles, deep, 8 * LANES), bf16),
            pltpu.VMEM((blocks, slots), f32),
            pltpu.VMEM((blocks, slots), i32),
            pltpu.VMEM((blocks, slots), i32),
            pltpu.VMEM((blocks, slots), i32),
            pltpu.VMEM((blocks, slots), i32),
            pltpu.VMEM((8 * deep, wide), bf16),
            pltpu.VMEM((3, deep, wide), f32),
            pltpu.VMEM((deep, wide), f32),
            pltpu.VMEM((4, blocks, slots), f32),
            pltpu.VMEM((tiles, 4, 4, 8, wide), f32),
            pltpu.VMEM((3, blocks, slots), f32),
            pltpu.VMEM((12 * rim, wide), f32),
            pltpu.VMEM((6 * mid, wide), f32),
            pltpu.VMEM((2, 4, rim, LANES), f32),
            pltpu.VMEM((2, 4, rim, LANES), f32),
            pltpu.VMEM((ITERS, 3, 2 * rim, wide), f32),
            pltpu.VMEM((ITERS, 3, 2 * rim, wide), f32),
            pltpu.VMEM((ITERS, 3, mid, wide), f32),
            pltpu.VMEM((ITERS, 3, mid, wide), f32),
            pltpu.VMEM((ITERS, 2, 3, 2 * rim, LANES), f32),
            pltpu.VMEM((ITERS, 2, 3, 2 * rim, LANES), f32),
            dma((2,)),
            dma((2,)),
            dma((ITERS,)),
            dma((ITERS,)),
            dma((ITERS,)),
            dma((ITERS,)),
            dma((ITERS, 2)),
            dma((ITERS, 2)),
        ],
        compiler_params=pltpu.CompilerParams(
            collective_id=0, has_side_effects=True, vmem_limit_bytes=40 * 1024 * 1024
        ),
    )(
        counts,
        v_free.reshape(3, rows, LANES),
        inv_mass.reshape(rows, LANES),
        pairs, angles, bias, friction,
    )
    return velocity.reshape(3, width), impulses


def solution(mesh):
    return jax.shard_map(
        functools.partial(on_device, mesh.shape["grp"]),
        mesh=mesh,
        in_specs=(
            P(None, "grp"),
            P("grp"),
            P(None, ("cell", "grp"), None),
            P(None, ("cell", "grp"), None),
            P(("cell", "grp"), None),
            P(("cell", "grp"), None),
            P(("cell", "grp")),
        ),
        out_specs=(P(None, "grp"), P(None, ("cell", "grp"), None)),
        check_vma=False,
    )
```

```python
import functools

import jax
import jax.numpy as jnp
from jax import lax
from jax.experimental import pallas as pl
from jax.experimental.pallas import tpu as pltpu
from jax.sharding import PartitionSpec as P

RIM = 2048
ITERS = 3
LANES = 128

relax_factor = 0.6
tangent_floor = 0.05


def split_terms(value):
    high = value.astype(jnp.bfloat16)
    low = (value - high.astype(jnp.float32)).astype(jnp.bfloat16)
    return high, low


def kernel(
    cells,
    counts_ref, v_ref, mass_ref, pairs_ref, angles_ref, bias_ref, friction_ref,
    vel_out, imp_out,
    hot1, hot2, spot1, spot2, row1, row2, active,
    h1_ref, h2_ref, l1_ref, l2_ref,
    vb, vfree_all, mass_all, rel, partial, force_ref, acc_outer, acc_inner,
    edge_out, edge_in, outer, outer_in, inner, inner_in, bound_out, bound_in,
    edge_send, edge_recv, outer_send, outer_recv, inner_send, inner_recv, bound_send, bound_recv,
):
    rows = v_ref.shape[1]
    rim = RIM // LANES
    half = rows // 2
    deep = half + rim
    mid = half - rim
    tiles = pairs_ref.shape[1] // 8
    core = lax.axis_index("cell")
    cell = lax.axis_index("grp")
    has_prev = cell > 0
    has_next = cell < cells - 1
    present = (has_prev, has_next)
    steps = (-1, 1)

    barrier = pltpu.get_barrier_semaphore()
    pl.semaphore_signal(barrier, inc=1, device_id={"cell": 1 - core}, device_id_type=pl.DeviceIdType.MESH)
    for side in range(2):
        @pl.when(present[side])
        def _():
            pl.semaphore_signal(
                barrier, inc=1, device_id={"grp": cell + steps[side]}, device_id_type=pl.DeviceIdType.MESH
            )

    edge_out[0, 0:3] = v_ref[:, 0:rim]
    edge_out[0, 3] = mass_ref[0:rim]
    edge_out[1, 0:3] = v_ref[:, rows - rim:rows]
    edge_out[1, 3] = mass_ref[rows - rim:rows]
    for side in range(2):
        @pl.when(jnp.logical_not(present[side]))
        def _():
            edge_in[side] = jnp.zeros(edge_in.shape[1:], jnp.float32)
            for sweep in range(ITERS):
                bound_in[sweep, side] = jnp.zeros(bound_in.shape[2:], jnp.float32)

    def edge_copy(side):
        return pltpu.make_async_remote_copy(
            src_ref=edge_out.at[side], dst_ref=edge_in.at[1 - side],
            send_sem=edge_send.at[side], recv_sem=edge_recv.at[1 - side],
            device_id={"grp": cell + steps[side]}, device_id_type=pl.DeviceIdType.MESH,
        )

    def outer_copy(sweep):
        return pltpu.make_async_remote_copy(
            src_ref=outer.at[sweep], dst_ref=outer_in.at[sweep],
            send_sem=outer_send.at[sweep], recv_sem=outer_recv.at[sweep],
            device_id={"cell": 1 - core}, device_id_type=pl.DeviceIdType.MESH,
        )

    def inner_copy(sweep):
        return pltpu.make_async_remote_copy(
            src_ref=inner.at[sweep], dst_ref=inner_in.at[sweep],
            send_sem=inner_send.at[sweep], recv_sem=inner_recv.at[sweep],
            device_id={"cell": 1 - core}, device_id_type=pl.DeviceIdType.MESH,
        )

    def bound_copy(sweep, side):
        size = rim if sweep == ITERS - 1 else 2 * rim
        return pltpu.make_async_remote_copy(
            src_ref=bound_out.at[sweep, side, :, pl.ds(0, size)],
            dst_ref=bound_in.at[sweep, 1 - side, :, pl.ds(0, size)],
            send_sem=bound_send.at[sweep, side], recv_sem=bound_recv.at[sweep, 1 - side],
            device_id={"grp": cell + steps[side]}, device_id_type=pl.DeviceIdType.MESH,
        )

    def place(position):
        own = position - RIM
        r = own >> 7
        lane = own & (LANES - 1)
        upper = r >= half
        h = jnp.where(upper, jnp.where(r >= rows - rim, r - (rows - rim), r - (half - rim)), r)
        l = jnp.where(upper, LANES, 0) + lane
        before = position < RIM
        after = own >= rows * LANES
        h = jnp.where(before, half + (position >> 7), jnp.where(after, half + r - rows, h))
        l = jnp.where(before, lane, jnp.where(after, LANES + lane, l))
        return h, l

    h1_ref[...], l1_ref[...] = place(pairs_ref[0])
    h2_ref[...], l2_ref[...] = place(pairs_ref[1])

    slot = lax.broadcasted_iota(jnp.int32, (1, LANES), 1)
    for r in range(pairs_ref.shape[1]):
        active[r:r + 1, :] = jnp.where(slot < counts_ref[r], 1.0, 0.0)

    def pair_row(tile, u):
        return jnp.concatenate([tile[2 * u:2 * u + 1], tile[2 * u + 1:2 * u + 2]], axis=1)

    wide = 2 * LANES
    iota_l = lax.broadcasted_iota(jnp.int32, (wide, wide), 0)
    iota_h = lax.broadcasted_iota(jnp.int32, (half, wide), 0)
    bf16 = jnp.bfloat16
    one, zero = jnp.ones((), bf16), jnp.zeros((), bf16)
    name_l = iota_l.astype(bf16)
    name_h = lax.broadcasted_iota(jnp.int32, (deep, wide), 0).astype(bf16)
    name_c = lax.broadcasted_iota(jnp.int32, (LANES, wide), 1).astype(bf16)

    def spread(line, size):
        return jnp.broadcast_to(line.astype(jnp.float32), (size,) + line.shape[1:]).astype(bf16)

    iota_o = lax.broadcasted_iota(jnp.int32, (rim, wide), 0)
    iota_m = lax.broadcasted_iota(jnp.int32, (mid, wide), 0) + rim
    iota_r = lax.broadcasted_iota(jnp.int32, (rim, wide), 0) + half

    sin_p, cos_p = jnp.sin(angles_ref[0]), jnp.cos(angles_ref[0])
    sin_q, cos_q = jnp.sin(angles_ref[1]), jnp.cos(angles_ref[1])
    normal = (sin_p * cos_q, sin_p * sin_q, cos_p)
    first_tan = (cos_p * cos_q, cos_p * sin_q, -sin_p)
    second_tan = (-sin_q, cos_q)

    def fold(block):
        lower = block[..., 0:half, :]
        upper = jnp.concatenate([block[..., rows - rim:rows, :], block[..., half:rows - rim, :]], axis=-2)
        return jnp.concatenate([lower, upper], axis=-1)

    vfree_all[:, 0:half] = fold(v_ref[...])
    mass_all[0:half] = fold(mass_ref[...])

    between = jnp.logical_and(has_prev, has_next)

    @pl.when(between)
    def _():
        pl.semaphore_wait(barrier, 3)

    @pl.when(jnp.logical_not(between))
    def _():
        pl.semaphore_wait(barrier, 2)

    for side in range(2):
        @pl.when(present[side])
        def _():
            edge_copy(side).start()

    def tile_at(i):
        return pl.ds(pl.multiple_of(i * 8, 8), 8)

    def store_terms(parts, base):
        count, size = len(parts), parts[0].shape[0]
        for c, part in enumerate(parts):
            for t, term in enumerate(split_terms(part)):
                at = base + (t * count + c) * size
                vb[at:at + size, :] = term

    def picked(g, base, size, c, count, mask, found=None):
        terms = []
        for t in range(2):
            at = base + (t * count + c) * size
            held = jnp.zeros((8, wide), jnp.float32) if found is None else found[t]
            for k in range(0, size, 8):
                held = jnp.where(mask[k:k + 8], g[at + k:at + k + 8], held)
            terms.append(held)
        return terms

    def gather_inner(count, fresh):
        @pl.loop(0, tiles)
        def _(i):
            h1, h2 = h1_ref[tile_at(i), :], h2_ref[tile_at(i), :]
            l1, l2 = l1_ref[tile_at(i), :], l2_ref[tile_at(i), :]
            for u in range(4):
                cut = slice(u * wide, (u + 1) * wide)
                h1_row, h2_row = pair_row(h1, u), pair_row(h2, u)
                if fresh:
                    hot1[i, :, cut] = jnp.where(name_l == spread(pair_row(l1, u), wide), one, zero)
                    hot2[i, :, cut] = jnp.where(name_l == spread(pair_row(l2, u), wide), one, zero)
                    for spot, l in ((spot1, l1), (spot2, l2)):
                        for s in (2 * u, 2 * u + 1):
                            lane_row = l[s:s + 1].astype(jnp.float32)
                            column = jnp.broadcast_to(lane_row, (LANES, LANES)).T.astype(bf16)
                            column = jnp.concatenate([column, column], axis=1)
                            spot[i, s * LANES:(s + 1) * LANES, :] = jnp.where(name_c == column, one, zero)
                    row1[i, :, cut] = jnp.where(name_h[0:half] == spread(h1_row, half), one, zero)
                    row2[i, :, cut] = jnp.where(name_h == spread(h2_row, deep), one, zero)
                source = vb[0:2 * count * mid, :]
                g1 = jnp.dot(source, hot1[i, :, cut], preferred_element_type=jnp.float32)
                g2 = jnp.dot(source, hot2[i, :, cut], preferred_element_type=jnp.float32)
                at1, at2 = iota_m == h1_row, iota_m == h2_row
                for c in range(count):
                    first = sum(picked(g1, 0, mid, c, count, at1))
                    second = sum(picked(g2, 0, mid, c, count, at2))
                    partial[i, u, c] = first + second if c == 3 else first - second

    def gather_outer(count):
        base = 2 * count * mid
        own = 2 * count * rim

        @pl.loop(0, tiles)
        def _(i):
            h1, h2 = h1_ref[tile_at(i), :], h2_ref[tile_at(i), :]
            found = [[] for _ in range(count)]
            for u in range(4):
                cut = slice(u * wide, (u + 1) * wide)
                h1_row, h2_row = pair_row(h1, u), pair_row(h2, u)
                g1 = jnp.dot(vb[base:base + own, :], hot1[i, :, cut], preferred_element_type=jnp.float32)
                g2 = jnp.dot(vb[base:base + 2 * own, :], hot2[i, :, cut], preferred_element_type=jnp.float32)
                at1, at2, at_rim = iota_o == h1_row, iota_o == h2_row, iota_r == h2_row
                for c in range(count):
                    first = sum(picked(g1, 0, rim, c, count, at1))
                    second = picked(g2, 0, rim, c, count, at2)
                    second = sum(picked(g2, own, rim, c, count, at_rim, second))
                    both_ends = partial[i, u, c] + (first + second if c == 3 else first - second)
                    line = jnp.sum(both_ends, axis=0, keepdims=True)
                    found[c] += [line[:, 0:LANES], line[:, LANES:wide]]
            for c in range(count):
                rel[c, tile_at(i), :] = jnp.concatenate(found[c], axis=0)

    def force_terms(i):
        pieces = []
        for c in range(3):
            tile = force_ref[c, tile_at(i), :]
            wide_row = jnp.concatenate([tile[s:s + 1] for s in range(8)], axis=1)
            pieces.append(split_terms(jnp.broadcast_to(wide_row, (16, 8 * LANES))))
        return pieces

    def weigh(mask, pieces, sign):
        size = mask.shape[0]
        done = []
        for t in range(2):
            for c in range(3):
                block = mask.reshape(size // 16, 16, 8 * LANES) * (sign * pieces[c][t])[None]
                done.append(block.reshape(size, 8 * LANES))
        return done

    def product(weighed, hot):
        return jnp.dot(jnp.concatenate(weighed, axis=0), hot, preferred_element_type=jnp.float32)

    def scatter_outer():
        acc_outer[...] = jnp.zeros(acc_outer.shape, jnp.float32)

        @pl.loop(0, tiles)
        def _(i):
            pieces = force_terms(i)
            mine = weigh(row1[i, 0:rim], pieces, 1)
            theirs = weigh(row2[i, 0:rim], pieces, -1) + weigh(row2[i, half:deep], pieces, -1)
            acc_outer[0:6 * rim, :] += product(mine, spot1[i])
            acc_outer[...] += product(theirs, spot2[i])

    def scatter_inner(begin, end):
        @pl.loop(begin, end)
        def _(i):
            pieces = force_terms(i)
            mine = product(weigh(row1[i, rim:half], pieces, 1), spot1[i])
            theirs = product(weigh(row2[i, rim:half], pieces, -1), spot2[i])
            acc_inner[...] += mine + theirs

    lambdas = [jnp.zeros(bias_ref.shape, jnp.float32)] * 3
    reduced = None
    for sweep in range(ITERS):
        last = sweep == ITERS - 1
        if sweep == 0:
            store_terms([vfree_all[c, rim:half] for c in range(3)] + [mass_all[rim:half]], 0)
            gather_inner(4, True)
            for side in range(2):
                @pl.when(present[side])
                def _():
                    edge_copy(1 - side).wait_recv()
            for side in range(2):
                cut = slice(side * LANES, (side + 1) * LANES)
                vfree_all[:, half:deep, cut] = edge_in[side, 0:3]
                mass_all[half:deep, cut] = edge_in[side, 3]
            base = 8 * mid
            store_terms([vfree_all[c, 0:rim] for c in range(3)] + [mass_all[0:rim]], base)
            store_terms([vfree_all[c, half:deep] for c in range(3)] + [mass_all[half:deep]], base + 8 * rim)
            gather_outer(4)
            reduced = relax_factor / rel[3]
        x, y, z = rel[0], rel[1], rel[2]
        speed_n = normal[0] * x + normal[1] * y + normal[2] * z + bias_ref[...]
        speed_a = first_tan[0] * x + first_tan[1] * y + first_tan[2] * z
        speed_b = second_tan[0] * x + second_tan[1] * y
        trial_n = lambdas[0] - reduced * speed_n
        trial_a = lambdas[1] - reduced * speed_a
        trial_b = lambdas[2] - reduced * speed_b
        normal_imp = jnp.maximum(trial_n, 0.0)
        tan_size = jnp.sqrt(trial_a * trial_a + trial_b * trial_b)
        factor = jnp.minimum(1.0, friction_ref[...] * normal_imp / jnp.maximum(tan_size, tangent_floor))
        live = active[...]
        lambdas = [normal_imp * live, trial_a * factor * live, trial_b * factor * live]
        for c in range(3):
            force = normal[c] * lambdas[0] + first_tan[c] * lambdas[1]
            if c < 2:
                force = force + second_tan[c] * lambdas[2]
            force_ref[c] = force

        early = max(1, tiles // 4 if last else tiles // 2)
        scatter_outer()
        for c in range(3):
            for part in range(2):
                a = (6 * part + c) * rim
                b = a + 3 * rim
                outer[sweep, c, part * rim:(part + 1) * rim] = acc_outer[a:a + rim, :] + acc_outer[b:b + rim, :]
        outer_copy(sweep).start()
        acc_inner[...] = jnp.zeros(acc_inner.shape, jnp.float32)
        scatter_inner(0, early)
        outer_copy(sweep).wait_recv()
        for side in range(2):
            cut = slice(side * LANES, (side + 1) * LANES)
            bound_out[sweep, side, :, 0:rim] = outer[sweep, :, rim:2 * rim, cut] + outer_in[sweep, :, rim:2 * rim, cut]
            bound_out[sweep, side, :, rim:2 * rim] = outer[sweep, :, 0:rim, cut] + outer_in[sweep, :, 0:rim, cut]
        for side in range(2):
            @pl.when(present[side])
            def _():
                bound_copy(sweep, side).start()
        scatter_inner(early, tiles)
        for c in range(3):
            a = c * mid
            b = a + 3 * mid
            inner[sweep, c] = acc_inner[a:a + mid, :] + acc_inner[b:b + mid, :]
        inner_copy(sweep).start()
        inner_copy(sweep).wait_recv()
        speeds = []
        for c in range(3):
            total = inner[sweep, c] + inner_in[sweep, c]
            speeds.append(vfree_all[c, rim:half] + mass_all[rim:half] * total)
        if last:
            for c in range(3):
                vel_out[c, rim:half] = speeds[c][:, 0:LANES]
                vel_out[c, half:rows - rim] = speeds[c][:, LANES:wide]
                imp_out[c] = lambdas[c]
        else:
            store_terms(speeds, 0)
            gather_inner(3, False)
        for side in range(2):
            @pl.when(present[side])
            def _():
                bound_copy(sweep, 1 - side).wait_recv()
        for part in range(1 if last else 2):
            here = slice((1 - part) * rim, (2 - part) * rim)
            there = slice(part * rim, (part + 1) * rim)
            body = slice(0, rim) if part == 0 else slice(half, deep)
            speeds = []
            for c in range(3):
                total = jnp.concatenate(
                    [bound_out[sweep, s, c, here] + bound_in[sweep, s, c, there] for s in range(2)], axis=-1
                )
                speeds.append(vfree_all[c, body] + mass_all[body] * total)
            if last:
                for c in range(3):
                    vel_out[c, 0:rim] = speeds[c][:, 0:LANES]
                    vel_out[c, rows - rim:rows] = speeds[c][:, LANES:wide]
            else:
                store_terms(speeds, 6 * mid + 6 * rim * part)
        if not last:
            gather_outer(3)
    for side in range(2):
        @pl.when(present[side])
        def _():
            edge_copy(side).wait_send()
            for sweep in range(ITERS):
                bound_copy(sweep, side).wait_send()
    for sweep in range(ITERS):
        outer_copy(sweep).wait_send()
        inner_copy(sweep).wait_send()


def on_device(cells, v_free, inv_mass, pairs, angles, bias, friction, counts):
    width = v_free.shape[1]
    blocks, slots = bias.shape
    rows = width // LANES
    rim = RIM // LANES
    half = rows // 2
    deep = half + rim
    mid = half - rim
    tiles = blocks // 8
    wide = 2 * LANES
    f32, bf16, i32 = jnp.float32, jnp.bfloat16, jnp.int32
    vmem = pl.BlockSpec(memory_space=pltpu.VMEM)
    dma = pltpu.SemaphoreType.DMA
    velocity, impulses = pl.pallas_call(
        functools.partial(kernel, cells),
        out_shape=(
            jax.ShapeDtypeStruct((3, rows, LANES), f32),
            jax.ShapeDtypeStruct((3, blocks, slots), f32),
        ),
        in_specs=[pl.BlockSpec(memory_space=pltpu.SMEM)] + [vmem] * 6,
        out_specs=(vmem, vmem),
        scratch_shapes=[
            pltpu.VMEM((tiles, wide, 8 * LANES), bf16),
            pltpu.VMEM((tiles, wide, 8 * LANES), bf16),
            pltpu.VMEM((tiles, 8 * LANES, wide), bf16),
            pltpu.VMEM((tiles, 8 * LANES, wide), bf16),
            pltpu.VMEM((tiles, half, 8 * LANES), bf16),
            pltpu.VMEM((tiles, deep, 8 * LANES), bf16),
            pltpu.VMEM((blocks, slots), f32),
            pltpu.VMEM((blocks, slots), i32),
            pltpu.VMEM((blocks, slots), i32),
            pltpu.VMEM((blocks, slots), i32),
            pltpu.VMEM((blocks, slots), i32),
            pltpu.VMEM((8 * deep, wide), bf16),
            pltpu.VMEM((3, deep, wide), f32),
            pltpu.VMEM((deep, wide), f32),
            pltpu.VMEM((4, blocks, slots), f32),
            pltpu.VMEM((tiles, 4, 4, 8, wide), f32),
            pltpu.VMEM((3, blocks, slots), f32),
            pltpu.VMEM((12 * rim, wide), f32),
            pltpu.VMEM((6 * mid, wide), f32),
            pltpu.VMEM((2, 4, rim, LANES), f32),
            pltpu.VMEM((2, 4, rim, LANES), f32),
            pltpu.VMEM((ITERS, 3, 2 * rim, wide), f32),
            pltpu.VMEM((ITERS, 3, 2 * rim, wide), f32),
            pltpu.VMEM((ITERS, 3, mid, wide), f32),
            pltpu.VMEM((ITERS, 3, mid, wide), f32),
            pltpu.VMEM((ITERS, 2, 3, 2 * rim, LANES), f32),
            pltpu.VMEM((ITERS, 2, 3, 2 * rim, LANES), f32),
            dma((2,)),
            dma((2,)),
            dma((ITERS,)),
            dma((ITERS,)),
            dma((ITERS,)),
            dma((ITERS,)),
            dma((ITERS, 2)),
            dma((ITERS, 2)),
        ],
        compiler_params=pltpu.CompilerParams(
            collective_id=0, has_side_effects=True, vmem_limit_bytes=40 * 1024 * 1024
        ),
    )(
        counts,
        v_free.reshape(3, rows, LANES),
        inv_mass.reshape(rows, LANES),
        pairs, angles, bias, friction,
    )
    return velocity.reshape(3, width), impulses


def solution(mesh):
    return jax.shard_map(
        functools.partial(on_device, mesh.shape["grp"]),
        mesh=mesh,
        in_specs=(
            P(None, "grp"),
            P("grp"),
            P(None, ("cell", "grp"), None),
            P(None, ("cell", "grp"), None),
            P(("cell", "grp"), None),
            P(("cell", "grp"), None),
            P(("cell", "grp")),
        ),
        out_specs=(P(None, "grp"), P(None, ("cell", "grp"), None)),
        check_vma=False,
    )
```

```python
import functools

import jax
import jax.numpy as jnp
from jax import lax
from jax.experimental import pallas as pl
from jax.experimental.pallas import tpu as pltpu
from jax.sharding import PartitionSpec as P

RIM = 2048
ITERS = 3
LANES = 128

relax_factor = 0.6
tangent_floor = 0.05


def split_terms(value):
    high = value.astype(jnp.bfloat16)
    low = (value - high.astype(jnp.float32)).astype(jnp.bfloat16)
    return high, low


def kernel(
    cells,
    counts_ref, v_ref, mass_ref, pairs_ref, angles_ref, bias_ref, friction_ref,
    vel_out, imp_out,
    spot1, spot2, row1, row2, active,
    h1_ref, h2_ref, l1_ref, l2_ref,
    table, vfree_all, mass_all, force_ref, acc_outer, acc_inner,
    edge_out, edge_in, outer, outer_in, inner, inner_in, bound_out, bound_in,
    edge_send, edge_recv, outer_send, outer_recv, inner_send, inner_recv, bound_send, bound_recv,
):
    rows = v_ref.shape[1]
    rim = RIM // LANES
    half = rows // 2
    deep = half + rim
    mid = half - rim
    tiles = pairs_ref.shape[1] // 8
    core = lax.axis_index("cell")
    cell = lax.axis_index("grp")
    has_prev = cell > 0
    has_next = cell < cells - 1
    present = (has_prev, has_next)
    steps = (-1, 1)

    barrier = pltpu.get_barrier_semaphore()
    pl.semaphore_signal(barrier, inc=1, device_id={"cell": 1 - core}, device_id_type=pl.DeviceIdType.MESH)
    for side in range(2):
        @pl.when(present[side])
        def _():
            pl.semaphore_signal(
                barrier, inc=1, device_id={"grp": cell + steps[side]}, device_id_type=pl.DeviceIdType.MESH
            )

    edge_out[0, 0:3] = v_ref[:, 0:rim]
    edge_out[0, 3] = mass_ref[0:rim]
    edge_out[1, 0:3] = v_ref[:, rows - rim:rows]
    edge_out[1, 3] = mass_ref[rows - rim:rows]
    for side in range(2):
        @pl.when(jnp.logical_not(present[side]))
        def _():
            edge_in[side] = jnp.zeros(edge_in.shape[1:], jnp.float32)
            for sweep in range(ITERS):
                bound_in[sweep, side] = jnp.zeros(bound_in.shape[2:], jnp.float32)

    def edge_copy(side):
        return pltpu.make_async_remote_copy(
            src_ref=edge_out.at[side], dst_ref=edge_in.at[1 - side],
            send_sem=edge_send.at[side], recv_sem=edge_recv.at[1 - side],
            device_id={"grp": cell + steps[side]}, device_id_type=pl.DeviceIdType.MESH,
        )

    def outer_copy(sweep):
        return pltpu.make_async_remote_copy(
            src_ref=outer.at[sweep], dst_ref=outer_in.at[sweep],
            send_sem=outer_send.at[sweep], recv_sem=outer_recv.at[sweep],
            device_id={"cell": 1 - core}, device_id_type=pl.DeviceIdType.MESH,
        )

    def inner_copy(sweep):
        return pltpu.make_async_remote_copy(
            src_ref=inner.at[sweep], dst_ref=inner_in.at[sweep],
            send_sem=inner_send.at[sweep], recv_sem=inner_recv.at[sweep],
            device_id={"cell": 1 - core}, device_id_type=pl.DeviceIdType.MESH,
        )

    def bound_copy(sweep, side):
        size = rim if sweep == ITERS - 1 else 2 * rim
        return pltpu.make_async_remote_copy(
            src_ref=bound_out.at[sweep, side, :, pl.ds(0, size)],
            dst_ref=bound_in.at[sweep, 1 - side, :, pl.ds(0, size)],
            send_sem=bound_send.at[sweep, side], recv_sem=bound_recv.at[sweep, 1 - side],
            device_id={"grp": cell + steps[side]}, device_id_type=pl.DeviceIdType.MESH,
        )

    def place(position):
        own = position - RIM
        r = own >> 7
        lane = own & (LANES - 1)
        upper = r >= half
        h = jnp.where(upper, jnp.where(r >= rows - rim, r - (rows - rim), r - (half - rim)), r)
        l = jnp.where(upper, LANES, 0) + lane
        before = position < RIM
        after = own >= rows * LANES
        h = jnp.where(before, half + (position >> 7), jnp.where(after, half + r - rows, h))
        l = jnp.where(before, lane, jnp.where(after, LANES + lane, l))
        return h, l

    h1_ref[...], l1_ref[...] = place(pairs_ref[0])
    h2_ref[...], l2_ref[...] = place(pairs_ref[1])

    lines = [[pairs_ref[e, 8 * t:8 * t + 8] >> 7 for t in range(tiles)] for e in range(2)]
    lanes = [[pairs_ref[e, 8 * t:8 * t + 8] & (LANES - 1) for t in range(tiles)] for e in range(2)]

    slot = lax.broadcasted_iota(jnp.int32, (1, LANES), 1)
    for r in range(pairs_ref.shape[1]):
        active[r:r + 1, :] = jnp.where(slot < counts_ref[r], 1.0, 0.0)

    def pair_row(tile, u):
        return jnp.concatenate([tile[2 * u:2 * u + 1], tile[2 * u + 1:2 * u + 2]], axis=1)

    wide = 2 * LANES
    bf16 = jnp.bfloat16
    one, zero = jnp.ones((), bf16), jnp.zeros((), bf16)
    name_h = lax.broadcasted_iota(jnp.int32, (deep, wide), 0).astype(bf16)
    name_c = lax.broadcasted_iota(jnp.int32, (LANES, wide), 1).astype(bf16)

    def spread(line, size):
        return jnp.broadcast_to(line.astype(jnp.float32), (size,) + line.shape[1:]).astype(bf16)

    iota_o = lax.broadcasted_iota(jnp.int32, (rim, wide), 0)
    iota_m = lax.broadcasted_iota(jnp.int32, (mid, wide), 0) + rim
    iota_r = lax.broadcasted_iota(jnp.int32, (rim, wide), 0) + half

    sin_p, cos_p = jnp.sin(angles_ref[0]), jnp.cos(angles_ref[0])
    sin_q, cos_q = jnp.sin(angles_ref[1]), jnp.cos(angles_ref[1])
    normal = (sin_p * cos_q, sin_p * sin_q, cos_p)
    first_tan = (cos_p * cos_q, cos_p * sin_q, -sin_p)
    second_tan = (-sin_q, cos_q)

    span = rows + 2 * rim
    vfree_all[:, rim:rim + rows] = v_ref[...]
    mass_all[rim:rim + rows] = mass_ref[...]

    between = jnp.logical_and(has_prev, has_next)

    @pl.when(between)
    def _():
        pl.semaphore_wait(barrier, 3)

    @pl.when(jnp.logical_not(between))
    def _():
        pl.semaphore_wait(barrier, 2)

    for side in range(2):
        @pl.when(present[side])
        def _():
            edge_copy(side).start()

    def tile_at(i):
        return pl.ds(pl.multiple_of(i * 8, 8), 8)

    def make_tables():
        @pl.loop(0, tiles)
        def _(i):
            h1, h2 = h1_ref[tile_at(i), :], h2_ref[tile_at(i), :]
            l1, l2 = l1_ref[tile_at(i), :], l2_ref[tile_at(i), :]
            for u in range(4):
                cut = slice(u * wide, (u + 1) * wide)
                for spot, l in ((spot1, l1), (spot2, l2)):
                    for s in (2 * u, 2 * u + 1):
                        lane_row = l[s:s + 1].astype(jnp.float32)
                        column = jnp.broadcast_to(lane_row, (LANES, LANES)).T.astype(bf16)
                        column = jnp.concatenate([column, column], axis=1)
                        spot[i, s * LANES:(s + 1) * LANES, :] = jnp.where(name_c == column, one, zero)
                row1[i, :, cut] = jnp.where(name_h[0:half] == spread(pair_row(h1, u), half), one, zero)
                row2[i, :, cut] = jnp.where(name_h == spread(pair_row(h2, u), deep), one, zero)

    def gather(sources, begin, end, ends, found):
        def body(k, found):
            found = list(found)
            start = pl.multiple_of(k * 8, 8)
            blocks = [source[pl.ds(start, 8), :] for source in sources]
            for s in range(8):
                here = [[line == start + s for line in lines[e]] for e in ends]
                for c, block in enumerate(blocks):
                    row = jnp.broadcast_to(block[s:s + 1], (8, LANES))
                    for n, e in enumerate(ends):
                        for t in range(tiles):
                            value = jnp.take_along_axis(row, lanes[e][t], axis=1, mode="promise_in_bounds")
                            at = (c * 2 + e) * tiles + t
                            found[at] = jnp.where(here[n][t], value, found[at])
            return tuple(found)

        return lax.fori_loop(begin // 8, end // 8, body, tuple(found))

    def gather_inner(sources):
        found = [jnp.zeros((8, LANES), jnp.float32)] * (len(sources) * 2 * tiles)
        return gather(sources, 2 * rim, rows, (0, 1), found)

    def gather_outer(sources, found):
        found = gather(sources, rim, 2 * rim, (0, 1), found)
        found = gather(sources, rows, rows + rim, (0, 1), found)
        found = gather(sources, 0, rim, (1,), found)
        return gather(sources, rows + rim, span, (1,), found)

    def joined(found, c, e):
        at = (c * 2 + e) * tiles
        return jnp.concatenate(found[at:at + tiles], axis=0)

    def force_terms(i):
        pieces = []
        for c in range(3):
            tile = force_ref[c, tile_at(i), :]
            wide_row = jnp.concatenate([tile[s:s + 1] for s in range(8)], axis=1)
            pieces.append(split_terms(jnp.broadcast_to(wide_row, (16, 8 * LANES))))
        return pieces

    def weigh(mask, pieces, sign):
        size = mask.shape[0]
        done = []
        for t in range(2):
            for c in range(3):
                block = mask.reshape(size // 16, 16, 8 * LANES) * (sign * pieces[c][t])[None]
                done.append(block.reshape(size, 8 * LANES))
        return done

    def product(weighed, hot):
        return jnp.dot(jnp.concatenate(weighed, axis=0), hot, preferred_element_type=jnp.float32)

    def scatter_outer():
        acc_outer[...] = jnp.zeros(acc_outer.shape, jnp.float32)

        @pl.loop(0, tiles)
        def _(i):
            pieces = force_terms(i)
            mine = weigh(row1[i, 0:rim], pieces, 1)
            theirs = weigh(row2[i, 0:rim], pieces, -1) + weigh(row2[i, half:deep], pieces, -1)
            acc_outer[0:6 * rim, :] += product(mine, spot1[i])
            acc_outer[...] += product(theirs, spot2[i])

    def scatter_inner(begin, end):
        @pl.loop(begin, end)
        def _(i):
            pieces = force_terms(i)
            mine = product(weigh(row1[i, rim:half], pieces, 1), spot1[i])
            theirs = product(weigh(row2[i, rim:half], pieces, -1), spot2[i])
            acc_inner[...] += mine + theirs

    lambdas = [jnp.zeros(bias_ref.shape, jnp.float32)] * 3
    reduced = None
    for sweep in range(ITERS):
        last = sweep == ITERS - 1
        if sweep == 0:
            make_tables()
            sources = [vfree_all.at[c] for c in range(3)]
            found = gather_inner(sources)
            weight = gather_inner([mass_all])
            for side in range(2):
                @pl.when(present[side])
                def _():
                    edge_copy(1 - side).wait_recv()
            for side in range(2):
                cut = slice(side * (rim + rows), side * (rim + rows) + rim)
                vfree_all[:, cut] = edge_in[side, 0:3]
                mass_all[cut] = edge_in[side, 3]
            found = gather_outer(sources, found)
            weight = gather_outer([mass_all], weight)
            reduced = relax_factor / (joined(weight, 0, 0) + joined(weight, 0, 1))
        x, y, z = (joined(found, c, 0) - joined(found, c, 1) for c in range(3))
        speed_n = normal[0] * x + normal[1] * y + normal[2] * z + bias_ref[...]
        speed_a = first_tan[0] * x + first_tan[1] * y + first_tan[2] * z
        speed_b = second_tan[0] * x + second_tan[1] * y
        trial_n = lambdas[0] - reduced * speed_n
        trial_a = lambdas[1] - reduced * speed_a
        trial_b = lambdas[2] - reduced * speed_b
        normal_imp = jnp.maximum(trial_n, 0.0)
        tan_size = jnp.sqrt(trial_a * trial_a + trial_b * trial_b)
        factor = jnp.minimum(1.0, friction_ref[...] * normal_imp / jnp.maximum(tan_size, tangent_floor))
        live = active[...]
        lambdas = [normal_imp * live, trial_a * factor * live, trial_b * factor * live]
        for c in range(3):
            force = normal[c] * lambdas[0] + first_tan[c] * lambdas[1]
            if c < 2:
                force = force + second_tan[c] * lambdas[2]
            force_ref[c] = force

        early = max(1, tiles // 4 if last else tiles // 2)
        scatter_outer()
        for c in range(3):
            for part in range(2):
                a = (6 * part + c) * rim
                b = a + 3 * rim
                outer[sweep, c, part * rim:(part + 1) * rim] = acc_outer[a:a + rim, :] + acc_outer[b:b + rim, :]
        outer_copy(sweep).start()
        acc_inner[...] = jnp.zeros(acc_inner.shape, jnp.float32)
        scatter_inner(0, early)
        outer_copy(sweep).wait_recv()
        for side in range(2):
            cut = slice(side * LANES, (side + 1) * LANES)
            bound_out[sweep, side, :, 0:rim] = outer[sweep, :, rim:2 * rim, cut] + outer_in[sweep, :, rim:2 * rim, cut]
            bound_out[sweep, side, :, rim:2 * rim] = outer[sweep, :, 0:rim, cut] + outer_in[sweep, :, 0:rim, cut]
        for side in range(2):
            @pl.when(present[side])
            def _():
                bound_copy(sweep, side).start()
        scatter_inner(early, tiles)
        for c in range(3):
            a = c * mid
            b = a + 3 * mid
            inner[sweep, c] = acc_inner[a:a + mid, :] + acc_inner[b:b + mid, :]
        inner_copy(sweep).start()
        inner_copy(sweep).wait_recv()
        for c in range(3):
            total = inner[sweep, c] + inner_in[sweep, c]
            for side in range(2):
                at = slice(2 * rim + side * mid, 2 * rim + (side + 1) * mid)
                speed = vfree_all[c, at] + mass_all[at] * total[:, side * LANES:(side + 1) * LANES]
                if last:
                    vel_out[c, rim + side * mid:rim + (side + 1) * mid] = speed
                else:
                    table[c, at] = speed
        if last:
            for c in range(3):
                imp_out[c] = lambdas[c]
        else:
            sources = [table.at[c] for c in range(3)]
            found = gather_inner(sources)
        for side in range(2):
            @pl.when(present[side])
            def _():
                bound_copy(sweep, 1 - side).wait_recv()
        for side in range(2):
            total = bound_out[sweep, side, :, rim:2 * rim] + bound_in[sweep, side, :, 0:rim]
            at = slice(rim + side * (rows - rim), rim + side * (rows - rim) + rim)
            speed = vfree_all[:, at] + mass_all[at][None] * total
            if last:
                vel_out[:, side * (rows - rim):side * (rows - rim) + rim] = speed
            else:
                table[:, at] = speed
                total = bound_out[sweep, side, :, 0:rim] + bound_in[sweep, side, :, rim:2 * rim]
                at = slice(side * (rows + rim), side * (rows + rim) + rim)
                table[:, at] = vfree_all[:, at] + mass_all[at][None] * total
        if not last:
            found = gather_outer(sources, found)
    for side in range(2):
        @pl.when(present[side])
        def _():
            edge_copy(side).wait_send()
            for sweep in range(ITERS):
                bound_copy(sweep, side).wait_send()
    for sweep in range(ITERS):
        outer_copy(sweep).wait_send()
        inner_copy(sweep).wait_send()


def on_device(cells, v_free, inv_mass, pairs, angles, bias, friction, counts):
    width = v_free.shape[1]
    blocks, slots = bias.shape
    rows = width // LANES
    rim = RIM // LANES
    half = rows // 2
    deep = half + rim
    mid = half - rim
    tiles = blocks // 8
    wide = 2 * LANES
    f32, bf16, i32 = jnp.float32, jnp.bfloat16, jnp.int32
    vmem = pl.BlockSpec(memory_space=pltpu.VMEM)
    dma = pltpu.SemaphoreType.DMA
    velocity, impulses = pl.pallas_call(
        functools.partial(kernel, cells),
        out_shape=(
            jax.ShapeDtypeStruct((3, rows, LANES), f32),
            jax.ShapeDtypeStruct((3, blocks, slots), f32),
        ),
        in_specs=[pl.BlockSpec(memory_space=pltpu.SMEM)] + [vmem] * 6,
        out_specs=(vmem, vmem),
        scratch_shapes=[
            pltpu.VMEM((tiles, 8 * LANES, wide), bf16),
            pltpu.VMEM((tiles, 8 * LANES, wide), bf16),
            pltpu.VMEM((tiles, half, 8 * LANES), bf16),
            pltpu.VMEM((tiles, deep, 8 * LANES), bf16),
            pltpu.VMEM((blocks, slots), f32),
            pltpu.VMEM((blocks, slots), i32),
            pltpu.VMEM((blocks, slots), i32),
            pltpu.VMEM((blocks, slots), i32),
            pltpu.VMEM((blocks, slots), i32),
            pltpu.VMEM((3, 2 * deep, LANES), f32),
            pltpu.VMEM((3, 2 * deep, LANES), f32),
            pltpu.VMEM((2 * deep, LANES), f32),
            pltpu.VMEM((3, blocks, slots), f32),
            pltpu.VMEM((12 * rim, wide), f32),
            pltpu.VMEM((6 * mid, wide), f32),
            pltpu.VMEM((2, 4, rim, LANES), f32),
            pltpu.VMEM((2, 4, rim, LANES), f32),
            pltpu.VMEM((ITERS, 3, 2 * rim, wide), f32),
            pltpu.VMEM((ITERS, 3, 2 * rim, wide), f32),
            pltpu.VMEM((ITERS, 3, mid, wide), f32),
            pltpu.VMEM((ITERS, 3, mid, wide), f32),
            pltpu.VMEM((ITERS, 2, 3, 2 * rim, LANES), f32),
            pltpu.VMEM((ITERS, 2, 3, 2 * rim, LANES), f32),
            dma((2,)),
            dma((2,)),
            dma((ITERS,)),
            dma((ITERS,)),
            dma((ITERS,)),
            dma((ITERS,)),
            dma((ITERS, 2)),
            dma((ITERS, 2)),
        ],
        compiler_params=pltpu.CompilerParams(
            collective_id=0, has_side_effects=True, vmem_limit_bytes=40 * 1024 * 1024
        ),
    )(
        counts,
        v_free.reshape(3, rows, LANES),
        inv_mass.reshape(rows, LANES),
        pairs, angles, bias, friction,
    )
    return velocity.reshape(3, width), impulses


def solution(mesh):
    return jax.shard_map(
        functools.partial(on_device, mesh.shape["grp"]),
        mesh=mesh,
        in_specs=(
            P(None, "grp"),
            P("grp"),
            P(None, ("cell", "grp"), None),
            P(None, ("cell", "grp"), None),
            P(("cell", "grp"), None),
            P(("cell", "grp"), None),
            P(("cell", "grp")),
        ),
        out_specs=(P(None, "grp"), P(None, ("cell", "grp"), None)),
        check_vma=False,
    )
```

```python
import functools

import jax
import jax.numpy as jnp
from jax import lax
from jax.experimental import pallas as pl
from jax.experimental.pallas import tpu as pltpu
from jax.sharding import PartitionSpec as P

RIM = 2048
ITERS = 3
LANES = 128

relax_factor = 0.6
tangent_floor = 0.05


def split_terms(value):
    high = value.astype(jnp.bfloat16)
    low = (value - high.astype(jnp.float32)).astype(jnp.bfloat16)
    return high, low


def kernel(
    cells,
    counts_ref, v_ref, mass_ref, pairs_ref, angles_ref, bias_ref, friction_ref,
    vel_out, imp_out,
    hot1, hot2, spot1, spot2, row1, row2, active,
    h1_ref, h2_ref, l1_ref, l2_ref,
    vb, vfree_all, mass_all, rel, partial, force_ref, acc_outer, acc_inner,
    edge_out, edge_in, outer, outer_in, inner, inner_in, bound_out, bound_in,
    edge_send, edge_recv, outer_send, outer_recv, inner_send, inner_recv, bound_send, bound_recv,
):
    rows = v_ref.shape[1] // LANES
    rim = RIM // LANES
    half = rows // 2
    deep = half + rim
    mid = half - rim
    tiles = pairs_ref.shape[1] // 8
    core = lax.axis_index("cell")
    cell = lax.axis_index("grp")
    has_prev = cell > 0
    has_next = cell < cells - 1
    present = (has_prev, has_next)
    steps = (-1, 1)

    barrier = pltpu.get_barrier_semaphore()
    pl.semaphore_signal(barrier, inc=1, device_id={"cell": 1 - core}, device_id_type=pl.DeviceIdType.MESH)
    for side in range(2):
        @pl.when(present[side])
        def _():
            pl.semaphore_signal(
                barrier, inc=1, device_id={"grp": cell + steps[side]}, device_id_type=pl.DeviceIdType.MESH
            )

    free = v_ref[...].reshape(3, rows, LANES)
    edge_out[0, 0:3] = free[:, 0:rim]
    edge_out[0, 3] = mass_ref[0:rim]
    edge_out[1, 0:3] = free[:, rows - rim:rows]
    edge_out[1, 3] = mass_ref[rows - rim:rows]
    for side in range(2):
        @pl.when(jnp.logical_not(present[side]))
        def _():
            edge_in[side] = jnp.zeros(edge_in.shape[1:], jnp.float32)
            for sweep in range(ITERS):
                bound_in[sweep, side] = jnp.zeros(bound_in.shape[2:], jnp.float32)

    def edge_copy(side):
        return pltpu.make_async_remote_copy(
            src_ref=edge_out.at[side], dst_ref=edge_in.at[1 - side],
            send_sem=edge_send.at[side], recv_sem=edge_recv.at[1 - side],
            device_id={"grp": cell + steps[side]}, device_id_type=pl.DeviceIdType.MESH,
        )

    def outer_copy(sweep):
        return pltpu.make_async_remote_copy(
            src_ref=outer.at[sweep], dst_ref=outer_in.at[sweep],
            send_sem=outer_send.at[sweep], recv_sem=outer_recv.at[sweep],
            device_id={"cell": 1 - core}, device_id_type=pl.DeviceIdType.MESH,
        )

    def inner_copy(sweep):
        return pltpu.make_async_remote_copy(
            src_ref=inner.at[sweep], dst_ref=inner_in.at[sweep],
            send_sem=inner_send.at[sweep], recv_sem=inner_recv.at[sweep],
            device_id={"cell": 1 - core}, device_id_type=pl.DeviceIdType.MESH,
        )

    def bound_copy(sweep, side):
        size = rim if sweep == ITERS - 1 else 2 * rim
        return pltpu.make_async_remote_copy(
            src_ref=bound_out.at[sweep, side, :, pl.ds(0, size)],
            dst_ref=bound_in.at[sweep, 1 - side, :, pl.ds(0, size)],
            send_sem=bound_send.at[sweep, side], recv_sem=bound_recv.at[sweep, 1 - side],
            device_id={"grp": cell + steps[side]}, device_id_type=pl.DeviceIdType.MESH,
        )

    def place(position):
        own = position - RIM
        r = own >> 7
        lane = own & (LANES - 1)
        upper = r >= half
        h = jnp.where(upper, jnp.where(r >= rows - rim, r - (rows - rim), r - (half - rim)), r)
        l = jnp.where(upper, LANES, 0) + lane
        before = position < RIM
        after = own >= rows * LANES
        h = jnp.where(before, half + (position >> 7), jnp.where(after, half + r - rows, h))
        l = jnp.where(before, lane, jnp.where(after, LANES + lane, l))
        return h, l

    h1_ref[...], l1_ref[...] = place(pairs_ref[0])
    h2_ref[...], l2_ref[...] = place(pairs_ref[1])

    slot = lax.broadcasted_iota(jnp.int32, (1, LANES), 1)
    for r in range(pairs_ref.shape[1]):
        active[r:r + 1, :] = jnp.where(slot < counts_ref[r], 1.0, 0.0)

    def pair_row(tile, u):
        return jnp.concatenate([tile[2 * u:2 * u + 1], tile[2 * u + 1:2 * u + 2]], axis=1)

    def quad_row(tile, u):
        return jnp.concatenate([tile[4 * u + n:4 * u + n + 1] for n in range(4)], axis=1)

    wide = 2 * LANES
    broad = 4 * LANES
    iota_l = lax.broadcasted_iota(jnp.int32, (wide, wide), 0)
    iota_h = lax.broadcasted_iota(jnp.int32, (half, wide), 0)
    bf16 = jnp.bfloat16
    one, zero = jnp.ones((), bf16), jnp.zeros((), bf16)
    name_l = iota_l.astype(bf16)
    name_h = lax.broadcasted_iota(jnp.int32, (deep, wide), 0).astype(bf16)
    name_c = lax.broadcasted_iota(jnp.int32, (LANES, wide), 1).astype(bf16)

    def spread(line, size):
        return jnp.broadcast_to(line.astype(jnp.float32), (size,) + line.shape[1:]).astype(bf16)

    iota_o = lax.broadcasted_iota(jnp.int32, (rim, broad), 0)
    iota_m = lax.broadcasted_iota(jnp.int32, (mid, broad), 0) + rim
    iota_r = lax.broadcasted_iota(jnp.int32, (rim, broad), 0) + half

    sin_p, cos_p = jnp.sin(angles_ref[0]), jnp.cos(angles_ref[0])
    sin_q, cos_q = jnp.sin(angles_ref[1]), jnp.cos(angles_ref[1])
    normal = (sin_p * cos_q, sin_p * sin_q, cos_p)
    first_tan = (cos_p * cos_q, cos_p * sin_q, -sin_p)
    second_tan = (-sin_q, cos_q)

    def fold(block):
        lower = block[..., 0:half, :]
        upper = jnp.concatenate([block[..., rows - rim:rows, :], block[..., half:rows - rim, :]], axis=-2)
        return jnp.concatenate([lower, upper], axis=-1)

    vfree_all[:, 0:half] = fold(free)
    mass_all[0:half] = fold(mass_ref[...])

    between = jnp.logical_and(has_prev, has_next)

    @pl.when(between)
    def _():
        pl.semaphore_wait(barrier, 3)

    @pl.when(jnp.logical_not(between))
    def _():
        pl.semaphore_wait(barrier, 2)

    for side in range(2):
        @pl.when(present[side])
        def _():
            edge_copy(side).start()

    def tile_at(i):
        return pl.ds(pl.multiple_of(i * 8, 8), 8)

    def store_terms(parts, base):
        count, size = len(parts), parts[0].shape[0]
        for c, part in enumerate(parts):
            for t, term in enumerate(split_terms(part)):
                at = base + (t * count + c) * size
                vb[at:at + size, :] = term

    def picked(g, base, size, c, count, mask, found=None):
        terms = []
        for t in range(2):
            at = base + (t * count + c) * size
            held = jnp.zeros((8, broad), jnp.float32) if found is None else found[t]
            for k in range(0, size, 8):
                held = jnp.where(mask[k:k + 8], g[at + k:at + k + 8], held)
            terms.append(held)
        return terms

    def gather_inner(count, fresh):
        @pl.loop(0, tiles)
        def _(i):
            h1, h2 = h1_ref[tile_at(i), :], h2_ref[tile_at(i), :]
            l1, l2 = l1_ref[tile_at(i), :], l2_ref[tile_at(i), :]
            for u in range(4):
                cut = slice(u * wide, (u + 1) * wide)
                h1_row, h2_row = pair_row(h1, u), pair_row(h2, u)
                if fresh:
                    hot1[i, :, cut] = jnp.where(name_l == spread(pair_row(l1, u), wide), one, zero)
                    hot2[i, :, cut] = jnp.where(name_l == spread(pair_row(l2, u), wide), one, zero)
                    for spot, l in ((spot1, l1), (spot2, l2)):
                        for s in (2 * u, 2 * u + 1):
                            lane_row = l[s:s + 1].astype(jnp.float32)
                            column = jnp.broadcast_to(lane_row, (LANES, LANES)).T.astype(bf16)
                            column = jnp.concatenate([column, column], axis=1)
                            spot[i, s * LANES:(s + 1) * LANES, :] = jnp.where(name_c == column, one, zero)
                    row1[i, :, cut] = jnp.where(name_h[0:half] == spread(h1_row, half), one, zero)
                    row2[i, :, cut] = jnp.where(name_h == spread(h2_row, deep), one, zero)
            source = vb[0:2 * count * mid, :]
            for u in range(2):
                cut = slice(u * broad, (u + 1) * broad)
                g1 = jnp.dot(source, hot1[i, :, cut], preferred_element_type=jnp.float32)
                g2 = jnp.dot(source, hot2[i, :, cut], preferred_element_type=jnp.float32)
                at1, at2 = iota_m == quad_row(h1, u), iota_m == quad_row(h2, u)
                for c in range(count):
                    first = sum(picked(g1, 0, mid, c, count, at1))
                    second = sum(picked(g2, 0, mid, c, count, at2))
                    partial[i, u, c] = first + second if c == 3 else first - second

    def gather_outer(count):
        base = 2 * count * mid
        own = 2 * count * rim

        @pl.loop(0, tiles)
        def _(i):
            h1, h2 = h1_ref[tile_at(i), :], h2_ref[tile_at(i), :]
            found = [[] for _ in range(count)]
            for u in range(2):
                cut = slice(u * broad, (u + 1) * broad)
                h1_row, h2_row = quad_row(h1, u), quad_row(h2, u)
                g1 = jnp.dot(vb[base:base + own, :], hot1[i, :, cut], preferred_element_type=jnp.float32)
                g2 = jnp.dot(vb[base:base + 2 * own, :], hot2[i, :, cut], preferred_element_type=jnp.float32)
                at1, at2, at_rim = iota_o == h1_row, iota_o == h2_row, iota_r == h2_row
                for c in range(count):
                    first = sum(picked(g1, 0, rim, c, count, at1))
                    second = picked(g2, 0, rim, c, count, at2)
                    second = sum(picked(g2, own, rim, c, count, at_rim, second))
                    both_ends = partial[i, u, c] + (first + second if c == 3 else first - second)
                    line = jnp.sum(both_ends, axis=0, keepdims=True)
                    found[c] += [line[:, n * LANES:(n + 1) * LANES] for n in range(4)]
            for c in range(count):
                rel[c, tile_at(i), :] = jnp.concatenate(found[c], axis=0)

    def force_terms(i):
        pieces = []
        for c in range(3):
            tile = force_ref[c, tile_at(i), :]
            wide_row = jnp.concatenate([tile[s:s + 1] for s in range(8)], axis=1)
            pieces.append(split_terms(jnp.broadcast_to(wide_row, (16, 8 * LANES))))
        return pieces

    def weigh(mask, pieces, sign):
        size = mask.shape[0]
        done = []
        for t in range(2):
            for c in range(3):
                block = mask.reshape(size // 16, 16, 8 * LANES) * (sign * pieces[c][t])[None]
                done.append(block.reshape(size, 8 * LANES))
        return done

    def product(weighed, hot):
        return jnp.dot(jnp.concatenate(weighed, axis=0), hot, preferred_element_type=jnp.float32)

    def scatter_outer():
        acc_outer[...] = jnp.zeros(acc_outer.shape, jnp.float32)

        @pl.loop(0, tiles)
        def _(i):
            pieces = force_terms(i)
            mine = weigh(row1[i, 0:rim], pieces, 1)
            theirs = weigh(row2[i, 0:rim], pieces, -1) + weigh(row2[i, half:deep], pieces, -1)
            acc_outer[0:6 * rim, :] += product(mine, spot1[i])
            acc_outer[...] += product(theirs, spot2[i])

    def scatter_inner(begin, end):
        @pl.loop(begin, end)
        def _(i):
            pieces = force_terms(i)
            mine = product(weigh(row1[i, rim:half], pieces, 1), spot1[i])
            theirs = product(weigh(row2[i, rim:half], pieces, -1), spot2[i])
            acc_inner[...] += mine + theirs

    lambdas = [jnp.zeros(bias_ref.shape, jnp.float32)] * 3
    reduced = None
    for sweep in range(ITERS):
        last = sweep == ITERS - 1
        if sweep == 0:
            store_terms([vfree_all[c, rim:half] for c in range(3)] + [mass_all[rim:half]], 0)
            gather_inner(4, True)
            for side in range(2):
                @pl.when(present[side])
                def _():
                    edge_copy(1 - side).wait_recv()
            for side in range(2):
                cut = slice(side * LANES, (side + 1) * LANES)
                vfree_all[:, half:deep, cut] = edge_in[side, 0:3]
                mass_all[half:deep, cut] = edge_in[side, 3]
            base = 8 * mid
            store_terms([vfree_all[c, 0:rim] for c in range(3)] + [mass_all[0:rim]], base)
            store_terms([vfree_all[c, half:deep] for c in range(3)] + [mass_all[half:deep]], base + 8 * rim)
            gather_outer(4)
            reduced = relax_factor / rel[3]
        x, y, z = rel[0], rel[1], rel[2]
        speed_n = normal[0] * x + normal[1] * y + normal[2] * z + bias_ref[...]
        speed_a = first_tan[0] * x + first_tan[1] * y + first_tan[2] * z
        speed_b = second_tan[0] * x + second_tan[1] * y
        trial_n = lambdas[0] - reduced * speed_n
        trial_a = lambdas[1] - reduced * speed_a
        trial_b = lambdas[2] - reduced * speed_b
        normal_imp = jnp.maximum(trial_n, 0.0)
        tan_size = jnp.sqrt(trial_a * trial_a + trial_b * trial_b)
        factor = jnp.minimum(1.0, friction_ref[...] * normal_imp / jnp.maximum(tan_size, tangent_floor))
        live = active[...]
        lambdas = [normal_imp * live, trial_a * factor * live, trial_b * factor * live]
        for c in range(3):
            force = normal[c] * lambdas[0] + first_tan[c] * lambdas[1]
            if c < 2:
                force = force + second_tan[c] * lambdas[2]
            force_ref[c] = force

        early = max(1, tiles // 4 if last else tiles // 2)
        scatter_outer()
        for c in range(3):
            for part in range(2):
                a = (6 * part + c) * rim
                b = a + 3 * rim
                outer[sweep, c, part * rim:(part + 1) * rim] = acc_outer[a:a + rim, :] + acc_outer[b:b + rim, :]
        outer_copy(sweep).start()
        acc_inner[...] = jnp.zeros(acc_inner.shape, jnp.float32)
        scatter_inner(0, early)
        outer_copy(sweep).wait_recv()
        for side in range(2):
            cut = slice(side * LANES, (side + 1) * LANES)
            bound_out[sweep, side, :, 0:rim] = outer[sweep, :, rim:2 * rim, cut] + outer_in[sweep, :, rim:2 * rim, cut]
            bound_out[sweep, side, :, rim:2 * rim] = outer[sweep, :, 0:rim, cut] + outer_in[sweep, :, 0:rim, cut]
        for side in range(2):
            @pl.when(present[side])
            def _():
                bound_copy(sweep, side).start()
        scatter_inner(early, tiles)
        for c in range(3):
            a = c * mid
            b = a + 3 * mid
            inner[sweep, c] = acc_inner[a:a + mid, :] + acc_inner[b:b + mid, :]
        inner_copy(sweep).start()
        inner_copy(sweep).wait_recv()
        speeds = []
        for c in range(3):
            total = inner[sweep, c] + inner_in[sweep, c]
            speeds.append(vfree_all[c, rim:half] + mass_all[rim:half] * total)
        if last:
            for c in range(3):
                vel_out[c, rim:half] = speeds[c][:, 0:LANES]
                vel_out[c, half:rows - rim] = speeds[c][:, LANES:wide]
                imp_out[c] = lambdas[c]
        else:
            store_terms(speeds, 0)
            gather_inner(3, False)
        for side in range(2):
            @pl.when(present[side])
            def _():
                bound_copy(sweep, 1 - side).wait_recv()
        for part in range(1 if last else 2):
            here = slice((1 - part) * rim, (2 - part) * rim)
            there = slice(part * rim, (part + 1) * rim)
            body = slice(0, rim) if part == 0 else slice(half, deep)
            speeds = []
            for c in range(3):
                total = jnp.concatenate(
                    [bound_out[sweep, s, c, here] + bound_in[sweep, s, c, there] for s in range(2)], axis=-1
                )
                speeds.append(vfree_all[c, body] + mass_all[body] * total)
            if last:
                for c in range(3):
                    vel_out[c, 0:rim] = speeds[c][:, 0:LANES]
                    vel_out[c, rows - rim:rows] = speeds[c][:, LANES:wide]
            else:
                store_terms(speeds, 6 * mid + 6 * rim * part)
        if not last:
            gather_outer(3)
    for side in range(2):
        @pl.when(present[side])
        def _():
            edge_copy(side).wait_send()
            for sweep in range(ITERS):
                bound_copy(sweep, side).wait_send()
    for sweep in range(ITERS):
        outer_copy(sweep).wait_send()
        inner_copy(sweep).wait_send()


def on_device(cells, v_free, inv_mass, pairs, angles, bias, friction, counts):
    width = v_free.shape[1]
    blocks, slots = bias.shape
    rows = width // LANES
    rim = RIM // LANES
    half = rows // 2
    deep = half + rim
    mid = half - rim
    tiles = blocks // 8
    wide = 2 * LANES
    f32, bf16, i32 = jnp.float32, jnp.bfloat16, jnp.int32
    vmem = pl.BlockSpec(memory_space=pltpu.VMEM)
    dma = pltpu.SemaphoreType.DMA
    velocity, impulses = pl.pallas_call(
        functools.partial(kernel, cells),
        out_shape=(
            jax.ShapeDtypeStruct((3, rows, LANES), f32),
            jax.ShapeDtypeStruct((3, blocks, slots), f32),
        ),
        in_specs=[pl.BlockSpec(memory_space=pltpu.SMEM)] + [vmem] * 6,
        out_specs=(vmem, vmem),
        scratch_shapes=[
            pltpu.VMEM((tiles, wide, 8 * LANES), bf16),
            pltpu.VMEM((tiles, wide, 8 * LANES), bf16),
            pltpu.VMEM((tiles, 8 * LANES, wide), bf16),
            pltpu.VMEM((tiles, 8 * LANES, wide), bf16),
            pltpu.VMEM((tiles, half, 8 * LANES), bf16),
            pltpu.VMEM((tiles, deep, 8 * LANES), bf16),
            pltpu.VMEM((blocks, slots), f32),
            pltpu.VMEM((blocks, slots), i32),
            pltpu.VMEM((blocks, slots), i32),
            pltpu.VMEM((blocks, slots), i32),
            pltpu.VMEM((blocks, slots), i32),
            pltpu.VMEM((8 * deep, wide), bf16),
            pltpu.VMEM((3, deep, wide), f32),
            pltpu.VMEM((deep, wide), f32),
            pltpu.VMEM((4, blocks, slots), f32),
            pltpu.VMEM((tiles, 2, 4, 8, 2 * wide), f32),
            pltpu.VMEM((3, blocks, slots), f32),
            pltpu.VMEM((12 * rim, wide), f32),
            pltpu.VMEM((6 * mid, wide), f32),
            pltpu.VMEM((2, 4, rim, LANES), f32),
            pltpu.VMEM((2, 4, rim, LANES), f32),
            pltpu.VMEM((ITERS, 3, 2 * rim, wide), f32),
            pltpu.VMEM((ITERS, 3, 2 * rim, wide), f32),
            pltpu.VMEM((ITERS, 3, mid, wide), f32),
            pltpu.VMEM((ITERS, 3, mid, wide), f32),
            pltpu.VMEM((ITERS, 2, 3, 2 * rim, LANES), f32),
            pltpu.VMEM((ITERS, 2, 3, 2 * rim, LANES), f32),
            dma((2,)),
            dma((2,)),
            dma((ITERS,)),
            dma((ITERS,)),
            dma((ITERS,)),
            dma((ITERS,)),
            dma((ITERS, 2)),
            dma((ITERS, 2)),
        ],
        compiler_params=pltpu.CompilerParams(
            collective_id=0, has_side_effects=True, vmem_limit_bytes=40 * 1024 * 1024
        ),
    )(
        counts,
        v_free,
        inv_mass.reshape(rows, LANES),
        pairs, angles, bias, friction,
    )
    return velocity.reshape(3, width), impulses


def solution(mesh):
    return jax.shard_map(
        functools.partial(on_device, mesh.shape["grp"]),
        mesh=mesh,
        in_specs=(
            P(None, "grp"),
            P("grp"),
            P(None, ("cell", "grp"), None),
            P(None, ("cell", "grp"), None),
            P(("cell", "grp"), None),
            P(("cell", "grp"), None),
            P(("cell", "grp")),
        ),
        out_specs=(P(None, "grp"), P(None, ("cell", "grp"), None)),
        check_vma=False,
    )
```

```python
import functools

import jax
import jax.numpy as jnp
from jax import lax
from jax.experimental import pallas as pl
from jax.experimental.pallas import tpu as pltpu
from jax.sharding import PartitionSpec as P

RIM = 2048
ITERS = 3
LANES = 128

relax_factor = 0.6
tangent_floor = 0.05


def split_terms(value):
    high = value.astype(jnp.bfloat16)
    low = (value - high.astype(jnp.float32)).astype(jnp.bfloat16)
    return high, low


def kernel(
    cells,
    counts_ref, v_hbm, mass_hbm, pairs_hbm, angles_hbm, bias_hbm, friction_hbm,
    vel_hbm, imp_hbm,
    vel_out, imp_out, store_sems, v_ref, mass_ref, pairs_ref, angles_ref, bias_ref, friction_ref, load_sems,
    hot1, hot2, spot1, spot2, row1, row2, active,
    h1_ref, h2_ref, l1_ref, l2_ref,
    vb, vfree_all, mass_all, rel, partial, force_ref, acc_outer, acc_inner,
    edge_out, edge_in, outer, outer_in, inner, inner_in, bound_out, bound_in,
    edge_send, edge_recv, outer_send, outer_recv, inner_send, inner_recv, bound_send, bound_recv,
):
    rows = v_ref.shape[1] // LANES
    rim = RIM // LANES
    half = rows // 2
    deep = half + rim
    mid = half - rim
    tiles = pairs_ref.shape[1] // 8
    core = lax.axis_index("cell")
    cell = lax.axis_index("grp")
    has_prev = cell > 0
    has_next = cell < cells - 1
    present = (has_prev, has_next)
    steps = (-1, 1)

    barrier = pltpu.get_barrier_semaphore()
    pl.semaphore_signal(barrier, inc=1, device_id={"cell": 1 - core}, device_id_type=pl.DeviceIdType.MESH)
    for side in range(2):
        @pl.when(present[side])
        def _():
            pl.semaphore_signal(
                barrier, inc=1, device_id={"grp": cell + steps[side]}, device_id_type=pl.DeviceIdType.MESH
            )

    loads = [
        pltpu.make_async_copy(source, target, load_sems.at[n])
        for n, (source, target) in enumerate((
            (pairs_hbm, pairs_ref), (v_hbm, v_ref), (mass_hbm, mass_ref),
            (angles_hbm, angles_ref), (bias_hbm, bias_ref), (friction_hbm, friction_ref),
        ))
    ]
    stores = [
        pltpu.make_async_copy(imp_out, imp_hbm, store_sems.at[0]),
        pltpu.make_async_copy(
            vel_out.at[:, pl.ds(rim, rows - 2 * rim)], vel_hbm.at[:, pl.ds(rim, rows - 2 * rim)], store_sems.at[1]
        ),
    ] + [
        pltpu.make_async_copy(
            vel_out.at[:, pl.ds(start, rim)], vel_hbm.at[:, pl.ds(start, rim)], store_sems.at[2 + side]
        )
        for side, start in enumerate((0, rows - rim))
    ]
    for load in loads:
        load.start()
    for load in loads:
        load.wait()

    free = v_ref[...].reshape(3, rows, LANES)
    edge_out[0, 0:3] = free[:, 0:rim]
    edge_out[0, 3] = mass_ref[0:rim]
    edge_out[1, 0:3] = free[:, rows - rim:rows]
    edge_out[1, 3] = mass_ref[rows - rim:rows]
    for side in range(2):
        @pl.when(jnp.logical_not(present[side]))
        def _():
            edge_in[side] = jnp.zeros(edge_in.shape[1:], jnp.float32)
            for sweep in range(ITERS):
                bound_in[sweep, side] = jnp.zeros(bound_in.shape[2:], jnp.float32)

    def edge_copy(side):
        return pltpu.make_async_remote_copy(
            src_ref=edge_out.at[side], dst_ref=edge_in.at[1 - side],
            send_sem=edge_send.at[side], recv_sem=edge_recv.at[1 - side],
            device_id={"grp": cell + steps[side]}, device_id_type=pl.DeviceIdType.MESH,
        )

    def outer_copy(sweep):
        return pltpu.make_async_remote_copy(
            src_ref=outer.at[sweep], dst_ref=outer_in.at[sweep],
            send_sem=outer_send.at[sweep], recv_sem=outer_recv.at[sweep],
            device_id={"cell": 1 - core}, device_id_type=pl.DeviceIdType.MESH,
        )

    def inner_copy(sweep):
        return pltpu.make_async_remote_copy(
            src_ref=inner.at[sweep], dst_ref=inner_in.at[sweep],
            send_sem=inner_send.at[sweep], recv_sem=inner_recv.at[sweep],
            device_id={"cell": 1 - core}, device_id_type=pl.DeviceIdType.MESH,
        )

    def bound_copy(sweep, side):
        size = rim if sweep == ITERS - 1 else 2 * rim
        return pltpu.make_async_remote_copy(
            src_ref=bound_out.at[sweep, side, :, pl.ds(0, size)],
            dst_ref=bound_in.at[sweep, 1 - side, :, pl.ds(0, size)],
            send_sem=bound_send.at[sweep, side], recv_sem=bound_recv.at[sweep, 1 - side],
            device_id={"grp": cell + steps[side]}, device_id_type=pl.DeviceIdType.MESH,
        )

    def place(position):
        own = position - RIM
        r = own >> 7
        lane = own & (LANES - 1)
        upper = r >= half
        h = jnp.where(upper, jnp.where(r >= rows - rim, r - (rows - rim), r - (half - rim)), r)
        l = jnp.where(upper, LANES, 0) + lane
        before = position < RIM
        after = own >= rows * LANES
        h = jnp.where(before, half + (position >> 7), jnp.where(after, half + r - rows, h))
        l = jnp.where(before, lane, jnp.where(after, LANES + lane, l))
        return h, l

    h1_ref[...], l1_ref[...] = place(pairs_ref[0])
    h2_ref[...], l2_ref[...] = place(pairs_ref[1])

    slot = lax.broadcasted_iota(jnp.int32, (1, LANES), 1)
    for r in range(pairs_ref.shape[1]):
        active[r:r + 1, :] = jnp.where(slot < counts_ref[r], 1.0, 0.0)

    def pair_row(tile, u):
        return jnp.concatenate([tile[2 * u:2 * u + 1], tile[2 * u + 1:2 * u + 2]], axis=1)

    def quad_row(tile, u):
        return jnp.concatenate([tile[4 * u + n:4 * u + n + 1] for n in range(4)], axis=1)

    wide = 2 * LANES
    broad = 4 * LANES
    iota_l = lax.broadcasted_iota(jnp.int32, (wide, wide), 0)
    iota_h = lax.broadcasted_iota(jnp.int32, (half, wide), 0)
    bf16 = jnp.bfloat16
    one, zero = jnp.ones((), bf16), jnp.zeros((), bf16)
    name_l = iota_l.astype(bf16)
    name_h = lax.broadcasted_iota(jnp.int32, (deep, wide), 0).astype(bf16)
    name_c = lax.broadcasted_iota(jnp.int32, (LANES, wide), 1).astype(bf16)

    def spread(line, size):
        return jnp.broadcast_to(line.astype(jnp.float32), (size,) + line.shape[1:]).astype(bf16)

    iota_o = lax.broadcasted_iota(jnp.int32, (rim, broad), 0)
    iota_m = lax.broadcasted_iota(jnp.int32, (mid, broad), 0) + rim
    iota_r = lax.broadcasted_iota(jnp.int32, (rim, broad), 0) + half

    sin_p, cos_p = jnp.sin(angles_ref[0]), jnp.cos(angles_ref[0])
    sin_q, cos_q = jnp.sin(angles_ref[1]), jnp.cos(angles_ref[1])
    normal = (sin_p * cos_q, sin_p * sin_q, cos_p)
    first_tan = (cos_p * cos_q, cos_p * sin_q, -sin_p)
    second_tan = (-sin_q, cos_q)

    def fold(block):
        lower = block[..., 0:half, :]
        upper = jnp.concatenate([block[..., rows - rim:rows, :], block[..., half:rows - rim, :]], axis=-2)
        return jnp.concatenate([lower, upper], axis=-1)

    vfree_all[:, 0:half] = fold(free)
    mass_all[0:half] = fold(mass_ref[...])

    between = jnp.logical_and(has_prev, has_next)

    @pl.when(between)
    def _():
        pl.semaphore_wait(barrier, 3)

    @pl.when(jnp.logical_not(between))
    def _():
        pl.semaphore_wait(barrier, 2)

    for side in range(2):
        @pl.when(present[side])
        def _():
            edge_copy(side).start()

    def tile_at(i):
        return pl.ds(pl.multiple_of(i * 8, 8), 8)

    def store_terms(parts, base):
        count, size = len(parts), parts[0].shape[0]
        for c, part in enumerate(parts):
            for t, term in enumerate(split_terms(part)):
                at = base + (t * count + c) * size
                vb[at:at + size, :] = term

    def picked(g, base, size, c, count, mask, found=None):
        terms = []
        for t in range(2):
            at = base + (t * count + c) * size
            held = jnp.zeros((8, broad), jnp.float32) if found is None else found[t]
            for k in range(0, size, 8):
                held = jnp.where(mask[k:k + 8], g[at + k:at + k + 8], held)
            terms.append(held)
        return terms

    def gather_inner(count, fresh):
        @pl.loop(0, tiles)
        def _(i):
            h1, h2 = h1_ref[tile_at(i), :], h2_ref[tile_at(i), :]
            l1, l2 = l1_ref[tile_at(i), :], l2_ref[tile_at(i), :]
            for u in range(4):
                cut = slice(u * wide, (u + 1) * wide)
                h1_row, h2_row = pair_row(h1, u), pair_row(h2, u)
                if fresh:
                    hot1[i, :, cut] = jnp.where(name_l == spread(pair_row(l1, u), wide), one, zero)
                    hot2[i, :, cut] = jnp.where(name_l == spread(pair_row(l2, u), wide), one, zero)
                    for spot, l in ((spot1, l1), (spot2, l2)):
                        for s in (2 * u, 2 * u + 1):
                            lane_row = l[s:s + 1].astype(jnp.float32)
                            column = jnp.broadcast_to(lane_row, (LANES, LANES)).T.astype(bf16)
                            column = jnp.concatenate([column, column], axis=1)
                            spot[i, s * LANES:(s + 1) * LANES, :] = jnp.where(name_c == column, one, zero)
                    row1[i, :, cut] = jnp.where(name_h[0:half] == spread(h1_row, half), one, zero)
                    row2[i, :, cut] = jnp.where(name_h == spread(h2_row, deep), one, zero)
            source = vb[0:2 * count * mid, :]
            for u in range(2):
                cut = slice(u * broad, (u + 1) * broad)
                g1 = jnp.dot(source, hot1[i, :, cut], preferred_element_type=jnp.float32)
                g2 = jnp.dot(source, hot2[i, :, cut], preferred_element_type=jnp.float32)
                at1, at2 = iota_m == quad_row(h1, u), iota_m == quad_row(h2, u)
                for c in range(count):
                    first = sum(picked(g1, 0, mid, c, count, at1))
                    second = sum(picked(g2, 0, mid, c, count, at2))
                    partial[i, u, c] = first + second if c == 3 else first - second

    def gather_outer(count):
        base = 2 * count * mid
        own = 2 * count * rim

        @pl.loop(0, tiles)
        def _(i):
            h1, h2 = h1_ref[tile_at(i), :], h2_ref[tile_at(i), :]
            found = [[] for _ in range(count)]
            for u in range(2):
                cut = slice(u * broad, (u + 1) * broad)
                h1_row, h2_row = quad_row(h1, u), quad_row(h2, u)
                g1 = jnp.dot(vb[base:base + own, :], hot1[i, :, cut], preferred_element_type=jnp.float32)
                g2 = jnp.dot(vb[base:base + 2 * own, :], hot2[i, :, cut], preferred_element_type=jnp.float32)
                at1, at2, at_rim = iota_o == h1_row, iota_o == h2_row, iota_r == h2_row
                for c in range(count):
                    first = sum(picked(g1, 0, rim, c, count, at1))
                    second = picked(g2, 0, rim, c, count, at2)
                    second = sum(picked(g2, own, rim, c, count, at_rim, second))
                    both_ends = partial[i, u, c] + (first + second if c == 3 else first - second)
                    line = jnp.sum(both_ends, axis=0, keepdims=True)
                    found[c] += [line[:, n * LANES:(n + 1) * LANES] for n in range(4)]
            for c in range(count):
                rel[c, tile_at(i), :] = jnp.concatenate(found[c], axis=0)

    def force_terms(i):
        pieces = []
        for c in range(3):
            tile = force_ref[c, tile_at(i), :]
            wide_row = jnp.concatenate([tile[s:s + 1] for s in range(8)], axis=1)
            pieces.append(split_terms(jnp.broadcast_to(wide_row, (16, 8 * LANES))))
        return pieces

    def weigh(mask, pieces, sign):
        size = mask.shape[0]
        done = []
        for t in range(2):
            for c in range(3):
                block = mask.reshape(size // 16, 16, 8 * LANES) * (sign * pieces[c][t])[None]
                done.append(block.reshape(size, 8 * LANES))
        return done

    def product(weighed, hot):
        return jnp.dot(jnp.concatenate(weighed, axis=0), hot, preferred_element_type=jnp.float32)

    def scatter_outer():
        acc_outer[...] = jnp.zeros(acc_outer.shape, jnp.float32)

        @pl.loop(0, tiles)
        def _(i):
            pieces = force_terms(i)
            mine = weigh(row1[i, 0:rim], pieces, 1)
            theirs = weigh(row2[i, 0:rim], pieces, -1) + weigh(row2[i, half:deep], pieces, -1)
            acc_outer[0:6 * rim, :] += product(mine, spot1[i])
            acc_outer[...] += product(theirs, spot2[i])

    def scatter_inner(begin, end):
        @pl.loop(begin, end)
        def _(i):
            pieces = force_terms(i)
            mine = product(weigh(row1[i, rim:half], pieces, 1), spot1[i])
            theirs = product(weigh(row2[i, rim:half], pieces, -1), spot2[i])
            acc_inner[...] += mine + theirs

    lambdas = [jnp.zeros(bias_ref.shape, jnp.float32)] * 3
    reduced = None
    for sweep in range(ITERS):
        last = sweep == ITERS - 1
        if sweep == 0:
            store_terms([vfree_all[c, rim:half] for c in range(3)] + [mass_all[rim:half]], 0)
            gather_inner(4, True)
            for side in range(2):
                @pl.when(present[side])
                def _():
                    edge_copy(1 - side).wait_recv()
            for side in range(2):
                cut = slice(side * LANES, (side + 1) * LANES)
                vfree_all[:, half:deep, cut] = edge_in[side, 0:3]
                mass_all[half:deep, cut] = edge_in[side, 3]
            base = 8 * mid
            store_terms([vfree_all[c, 0:rim] for c in range(3)] + [mass_all[0:rim]], base)
            store_terms([vfree_all[c, half:deep] for c in range(3)] + [mass_all[half:deep]], base + 8 * rim)
            gather_outer(4)
            reduced = relax_factor / rel[3]
        x, y, z = rel[0], rel[1], rel[2]
        speed_n = normal[0] * x + normal[1] * y + normal[2] * z + bias_ref[...]
        speed_a = first_tan[0] * x + first_tan[1] * y + first_tan[2] * z
        speed_b = second_tan[0] * x + second_tan[1] * y
        trial_n = lambdas[0] - reduced * speed_n
        trial_a = lambdas[1] - reduced * speed_a
        trial_b = lambdas[2] - reduced * speed_b
        normal_imp = jnp.maximum(trial_n, 0.0)
        tan_size = jnp.sqrt(trial_a * trial_a + trial_b * trial_b)
        factor = jnp.minimum(1.0, friction_ref[...] * normal_imp / jnp.maximum(tan_size, tangent_floor))
        live = active[...]
        lambdas = [normal_imp * live, trial_a * factor * live, trial_b * factor * live]
        for c in range(3):
            force = normal[c] * lambdas[0] + first_tan[c] * lambdas[1]
            if c < 2:
                force = force + second_tan[c] * lambdas[2]
            force_ref[c] = force

        early = max(1, tiles // 4)
        scatter_outer()
        for c in range(3):
            for part in range(2):
                a = (6 * part + c) * rim
                b = a + 3 * rim
                outer[sweep, c, part * rim:(part + 1) * rim] = acc_outer[a:a + rim, :] + acc_outer[b:b + rim, :]
        outer_copy(sweep).start()
        acc_inner[...] = jnp.zeros(acc_inner.shape, jnp.float32)
        scatter_inner(0, early)
        outer_copy(sweep).wait_recv()
        for side in range(2):
            cut = slice(side * LANES, (side + 1) * LANES)
            bound_out[sweep, side, :, 0:rim] = outer[sweep, :, rim:2 * rim, cut] + outer_in[sweep, :, rim:2 * rim, cut]
            bound_out[sweep, side, :, rim:2 * rim] = outer[sweep, :, 0:rim, cut] + outer_in[sweep, :, 0:rim, cut]
        for side in range(2):
            @pl.when(present[side])
            def _():
                bound_copy(sweep, side).start()
        scatter_inner(early, tiles)
        for c in range(3):
            a = c * mid
            b = a + 3 * mid
            inner[sweep, c] = acc_inner[a:a + mid, :] + acc_inner[b:b + mid, :]
        inner_copy(sweep).start()
        inner_copy(sweep).wait_recv()
        speeds = []
        for c in range(3):
            total = inner[sweep, c] + inner_in[sweep, c]
            speeds.append(vfree_all[c, rim:half] + mass_all[rim:half] * total)
        if last:
            for c in range(3):
                vel_out[c, rim:half] = speeds[c][:, 0:LANES]
                vel_out[c, half:rows - rim] = speeds[c][:, LANES:wide]
                imp_out[c] = lambdas[c]
            stores[0].start()
            stores[1].start()
        else:
            store_terms(speeds, 0)
            gather_inner(3, False)
        for side in range(2):
            @pl.when(present[side])
            def _():
                bound_copy(sweep, 1 - side).wait_recv()
        for part in range(1 if last else 2):
            here = slice((1 - part) * rim, (2 - part) * rim)
            there = slice(part * rim, (part + 1) * rim)
            body = slice(0, rim) if part == 0 else slice(half, deep)
            speeds = []
            for c in range(3):
                total = jnp.concatenate(
                    [bound_out[sweep, s, c, here] + bound_in[sweep, s, c, there] for s in range(2)], axis=-1
                )
                speeds.append(vfree_all[c, body] + mass_all[body] * total)
            if last:
                for c in range(3):
                    vel_out[c, 0:rim] = speeds[c][:, 0:LANES]
                    vel_out[c, rows - rim:rows] = speeds[c][:, LANES:wide]
            else:
                store_terms(speeds, 6 * mid + 6 * rim * part)
        if not last:
            gather_outer(3)
    stores[2].start()
    stores[3].start()
    for side in range(2):
        @pl.when(present[side])
        def _():
            edge_copy(side).wait_send()
            for sweep in range(ITERS):
                bound_copy(sweep, side).wait_send()
    for sweep in range(ITERS):
        outer_copy(sweep).wait_send()
        inner_copy(sweep).wait_send()
    for store in stores:
        store.wait()


def on_device(cells, v_free, inv_mass, pairs, angles, bias, friction, counts):
    width = v_free.shape[1]
    blocks, slots = bias.shape
    rows = width // LANES
    rim = RIM // LANES
    half = rows // 2
    deep = half + rim
    mid = half - rim
    tiles = blocks // 8
    wide = 2 * LANES
    f32, bf16, i32 = jnp.float32, jnp.bfloat16, jnp.int32
    dma = pltpu.SemaphoreType.DMA
    velocity, impulses = pl.pallas_call(
        functools.partial(kernel, cells),
        out_shape=(
            jax.ShapeDtypeStruct((3, rows, LANES), f32),
            jax.ShapeDtypeStruct((3, blocks, slots), f32),
        ),
        in_specs=[pl.BlockSpec(memory_space=pltpu.SMEM)] + [pl.BlockSpec(memory_space=pl.ANY)] * 6,
        out_specs=(pl.BlockSpec(memory_space=pl.ANY),) * 2,
        scratch_shapes=[
            pltpu.VMEM((3, rows, LANES), f32),
            pltpu.VMEM((3, blocks, slots), f32),
            dma((4,)),
            pltpu.VMEM((3, width), f32),
            pltpu.VMEM((rows, LANES), f32),
            pltpu.VMEM((2, blocks, slots), i32),
            pltpu.VMEM((2, blocks, slots), f32),
            pltpu.VMEM((blocks, slots), f32),
            pltpu.VMEM((blocks, slots), f32),
            dma((6,)),
            pltpu.VMEM((tiles, wide, 8 * LANES), bf16),
            pltpu.VMEM((tiles, wide, 8 * LANES), bf16),
            pltpu.VMEM((tiles, 8 * LANES, wide), bf16),
            pltpu.VMEM((tiles, 8 * LANES, wide), bf16),
            pltpu.VMEM((tiles, half, 8 * LANES), bf16),
            pltpu.VMEM((tiles, deep, 8 * LANES), bf16),
            pltpu.VMEM((blocks, slots), f32),
            pltpu.VMEM((blocks, slots), i32),
            pltpu.VMEM((blocks, slots), i32),
            pltpu.VMEM((blocks, slots), i32),
            pltpu.VMEM((blocks, slots), i32),
            pltpu.VMEM((8 * deep, wide), bf16),
            pltpu.VMEM((3, deep, wide), f32),
            pltpu.VMEM((deep, wide), f32),
            pltpu.VMEM((4, blocks, slots), f32),
            pltpu.VMEM((tiles, 2, 4, 8, 2 * wide), f32),
            pltpu.VMEM((3, blocks, slots), f32),
            pltpu.VMEM((12 * rim, wide), f32),
            pltpu.VMEM((6 * mid, wide), f32),
            pltpu.VMEM((2, 4, rim, LANES), f32),
            pltpu.VMEM((2, 4, rim, LANES), f32),
            pltpu.VMEM((ITERS, 3, 2 * rim, wide), f32),
            pltpu.VMEM((ITERS, 3, 2 * rim, wide), f32),
            pltpu.VMEM((ITERS, 3, mid, wide), f32),
            pltpu.VMEM((ITERS, 3, mid, wide), f32),
            pltpu.VMEM((ITERS, 2, 3, 2 * rim, LANES), f32),
            pltpu.VMEM((ITERS, 2, 3, 2 * rim, LANES), f32),
            dma((2,)),
            dma((2,)),
            dma((ITERS,)),
            dma((ITERS,)),
            dma((ITERS,)),
            dma((ITERS,)),
            dma((ITERS, 2)),
            dma((ITERS, 2)),
        ],
        compiler_params=pltpu.CompilerParams(
            collective_id=0, has_side_effects=True, vmem_limit_bytes=56 * 1024 * 1024
        ),
    )(
        counts,
        v_free,
        inv_mass.reshape(rows, LANES),
        pairs, angles, bias, friction,
    )
    return velocity.reshape(3, width), impulses


def solution(mesh):
    return jax.shard_map(
        functools.partial(on_device, mesh.shape["grp"]),
        mesh=mesh,
        in_specs=(
            P(None, "grp"),
            P("grp"),
            P(None, ("cell", "grp"), None),
            P(None, ("cell", "grp"), None),
            P(("cell", "grp"), None),
            P(("cell", "grp"), None),
            P(("cell", "grp")),
        ),
        out_specs=(P(None, "grp"), P(None, ("cell", "grp"), None)),
        check_vma=False,
    )
```
